128 devices in a mesh: uly: 4 (over x_lo, core), blk: 32 (over x_hi, z, y).
Axes of the slice: x: 4 (x_hi: 2, x_lo: 2; x = x_hi * 2 + x_lo), y: 4, z: 4, core: 2. Of those that a mesh axis runs over, the one named last changes fastest.
Arguments:
- queries: bfloat16 [12288, 2560], P(('blk', 'uly')), may hold values from -5 to 5
- key_rows: bfloat16 [12288, 2560], P(('blk', 'uly')), may hold values from -5 to 5
- value_rows: bfloat16 [12288, 2560], P(('blk', 'uly')), may hold values from -6 to 6
- block_list: int32 [20, 96, 16], replicated, may hold values from 0 to 95, as said below
- block_count: int32 [20, 96], replicated, may hold values from 1 to 16, as said below
- w_out: bfloat16 [2560, 5120], P('uly'), may hold values from -0.125 to 0.125
Outputs:
- projected: bfloat16 [12288, 5120], P(('blk', 'uly'))
The draws below stay inside these ranges and needn't reach their ends.
Inputs may be any that keep to these rules, and one draw needn't show every extreme that they name: `block_list`: each row of 16 entries holds distinct key block indices; its first entry is the row's own query block. `block_count`: some head and query block uses all 16 entries.
All inputs are finite; a program needn't handle non-finite values.
Results may differ from the reference program's by a relative error of at most 0.015.
Values may be sent and summed in bfloat16 or wider, within the bound.
No kernel may reach another device: no remote copies, remote signals or barrier semaphores. Data moves between devices by JAX's collectives and lax.ppermute only.
A program may use at most 384 MiB of HBM per device.

```python
import jax
import jax.numpy as jnp
from jax import lax

D = 5120
HEADS = 20
HEAD = 128
BLOCK = 128
MAXB = 16
HD = 2560
LENGTH = 12288
NB = 96


def draw_queries(key, part):
    key = jax.random.fold_in(key, 21)
    field = jnp.clip(jax.random.normal(key, (LENGTH, HD), jnp.float32), -5.0, 5.0)
    return field.astype(jnp.bfloat16)


def draw_key_rows(key, part):
    key = jax.random.fold_in(key, 22)
    field = jnp.clip(jax.random.normal(key, (LENGTH, HD), jnp.float32), -5.0, 5.0)
    return field.astype(jnp.bfloat16)


def draw_block_list(key, part):
    key = jax.random.fold_in(key, 31)
    row_total = HEADS * NB
    raw = jax.random.randint(key, (row_total, NB - 1), 0, 1048576)
    ranked = jnp.argsort(raw * NB + jnp.arange(NB - 1, dtype=jnp.int32)[None, :], axis=1).astype(jnp.int32)
    offsets = jnp.concatenate([jnp.zeros((row_total, 1), jnp.int32), ranked + 1], axis=1)[:, :MAXB]
    own_block = (jnp.arange(row_total, dtype=jnp.int32) % NB)[:, None]
    return ((own_block + offsets) % NB).reshape(HEADS, NB, MAXB).astype(jnp.int32)


def draw_block_count(key, part):
    key = jax.random.fold_in(key, 41)
    first_key, second_key, third_key = jax.random.split(key, 3)
    caps = jax.random.randint(first_key, (HEADS, 1), 6, MAXB + 1)
    lowest = caps // 2 + 1
    counts = lowest + jax.random.randint(second_key, (HEADS, NB), 0, 1048576) % (caps - lowest + 1)
    spot = jax.random.randint(third_key, (), 0, HEADS * NB)
    places = jnp.arange(HEADS * NB, dtype=jnp.int32).reshape(HEADS, NB)
    counts = jnp.where(places == spot, MAXB, counts)
    return counts.astype(jnp.int32)


def shard_levels(stream_key, extent, cuts, smallest, top_value):
    loudness = 1.0
    for dim, shards_of in cuts:
        heights = jax.random.uniform(jax.random.fold_in(jax.random.fold_in(stream_key, 6), dim), (shards_of,), jnp.float32, smallest / len(cuts), top_value / len(cuts))
        loudness = loudness * jnp.repeat(jnp.exp(heights), extent[dim] // shards_of).reshape((-1,) + (1,) * (len(extent) - 1 - dim))
    return loudness


def scatter_about(key, shape, scale, limit, cuts=(), kind=jnp.bfloat16):
    drawn = scale * jax.random.normal(key, shape, jnp.float32)
    if cuts:
        drawn = drawn * shard_levels(key, shape, cuts, -0.22, 0.18)
    return jnp.clip(drawn, -limit, limit).astype(kind)


def setup_inputs(seed: int = 0) -> dict:
    arg_keys = jax.random.split(jax.random.key(seed), 7)
    queries = draw_queries(jax.random.fold_in(arg_keys[6], 71), 0)
    key_rows = draw_key_rows(jax.random.fold_in(arg_keys[6], 71), 0)
    value_rows = scatter_about(arg_keys[2], (LENGTH, HD), 1.0, 6.0, ((0, 128),))
    block_list = draw_block_list(jax.random.fold_in(arg_keys[6], 71), 0)
    block_count = draw_block_count(jax.random.fold_in(arg_keys[6], 71), 0)
    w_out = scatter_about(arg_keys[5], (HD, D), HD ** -0.5, 0.125, ((0, 4),))
    return dict(queries=queries, key_rows=key_rows, value_rows=value_rows, block_list=block_list, block_count=block_count, w_out=w_out)


def reference(queries, key_rows, value_rows, block_list, block_count, w_out):
    block_total = LENGTH // BLOCK
    slot_live = jnp.arange(MAXB, dtype=jnp.int32)[None, None, :] < block_count[:, :, None]
    block_ids = jnp.arange(block_total, dtype=jnp.int32)
    block_mask = jnp.any((block_list[..., None] == block_ids) & slot_live[..., None], axis=2)
    scaling = HEAD ** -0.5

    def one_head(head):
        q_head = lax.dynamic_slice_in_dim(queries, head * HEAD, HEAD, 1)
        k_head = lax.dynamic_slice_in_dim(key_rows, head * HEAD, HEAD, 1)
        v_head = lax.dynamic_slice_in_dim(value_rows, head * HEAD, HEAD, 1)
        head_mask = block_mask[head]

        def one_block(block_idx):
            q_part = lax.dynamic_slice_in_dim(q_head, block_idx * BLOCK, BLOCK, 0)
            scores = jnp.dot(q_part, k_head.T, preferred_element_type=jnp.float32) * scaling
            allowed = jnp.repeat(head_mask[block_idx], BLOCK)
            scores = jnp.where(allowed[None, :], scores, -jnp.inf)
            row_max = jnp.max(scores, axis=1, keepdims=True)
            weights = jnp.exp(scores - row_max)
            row_sum = jnp.sum(weights, axis=1, keepdims=True)
            result = jnp.dot(weights.astype(jnp.bfloat16), v_head, preferred_element_type=jnp.float32) / row_sum
            return result.astype(jnp.bfloat16)

        blocks_out = lax.map(one_block, jnp.arange(block_total, dtype=jnp.int32))
        return blocks_out.reshape(LENGTH, HEAD)

    per_head = lax.map(one_head, jnp.arange(HEADS, dtype=jnp.int32))
    attended = per_head.transpose(1, 0, 2).reshape(LENGTH, HEADS * HEAD)
    return jnp.dot(attended, w_out, preferred_element_type=jnp.float32).astype(jnp.bfloat16)
```

```python
import functools

import jax
import jax.numpy as jnp
from jax import lax
from jax.experimental import pallas as pl
from jax.experimental.pallas import tpu as pltpu
from jax.sharding import Mesh, PartitionSpec as P

HEAD = 128
BLOCK = 128
ROWS = 96
CHUNKS = 4
SUPER = ROWS * CHUNKS
EXT = 32
HALF = 16
LOG2E = 1.4426950408889634
SCALE = HEAD ** -0.5 * LOG2E
FLOOR = -1e30
NAMES = ("xh", "zh", "zl", "y", "xl", "c")
GRID = ("xl", "c", "xh", "zh", "zl", "y")
SIZES = (2, 2, 2, 2, 2, 4)
SPREAD = ("xh", "zh", "xl", "c")
STATS = 16


def ring_up(x):
    return lax.ppermute(x, "y", [(i, (i + 1) % 4) for i in range(4)])


def ring_down(x):
    return lax.ppermute(x, "y", [(i, (i - 1) % 4) for i in range(4)])


def swap(x):
    return lax.ppermute(x, "zl", [(0, 1), (1, 0)])


def attention_kernel(
    where_ref, list_ref, count_ref, shared_list_ref, shared_count_ref, q_ref,
    a00, a01, am0, ap0, a11, am1, a20, last_k, last_v, last_e,
    out_ref, k_main, v_main, k_ext, v_ext, sem,
):
    y = where_ref[0]
    zl = where_ref[1]
    group = where_ref[2]
    copies = []

    def put(source, lo, rows, target, dy, dz):
        yy = lax.rem(y + (dy + 4), 4)
        zz = lax.rem(zl + dz, 2)
        copy = pltpu.make_async_copy(
            source.at[:, :, pl.ds(lo, rows)], target.at[:, zz, yy], sem.at[len(copies)]
        )
        copy.start()
        copies.append(copy)

    for source, dy, dz in (
        (a00, 0, 0), (a01, 0, 1), (am0, -1, 0), (ap0, 1, 0), (a11, 1, 1), (am1, -1, 1), (a20, 2, 0),
    ):
        put(source, 0, ROWS, k_main, dy, dz)
        put(source, ROWS, ROWS, v_main, dy, dz)
        put(source, 2 * ROWS, EXT, k_ext, dy, dz)
        put(source, 2 * ROWS + EXT, EXT, v_ext, dy, dz)
    put(last_k, 0, ROWS, k_main, 2, 1)
    put(last_v, 0, ROWS, v_main, 2, 1)
    put(last_e, 0, EXT, k_ext, 2, 1)
    put(last_e, EXT, EXT, v_ext, 2, 1)
    for copy in copies:
        copy.wait()

    k_flat = k_main.reshape(32 * SUPER, HEAD)
    v_flat = v_main.reshape(32 * SUPER, HEAD)
    ke_flat = k_ext.reshape(32 * CHUNKS * EXT, HEAD)
    ve_flat = v_ext.reshape(32 * CHUNKS * EXT, HEAD)
    col = lax.broadcasted_iota(jnp.int32, (BLOCK, 512), 1)
    eye = lax.broadcasted_iota(jnp.int32, (BLOCK, BLOCK), 0) == lax.broadcasted_iota(
        jnp.int32, (BLOCK, BLOCK), 1
    )

    def dot_t(a, b):
        return lax.dot_general(a, b, (((1,), (1,)), ((), ())), preferred_element_type=jnp.float32)

    def place(unit):
        sb = lax.div(unit, 3)
        return sb, pl.multiple_of((unit - 3 * sb) * BLOCK, BLOCK)

    def main_unit(unit, carry):
        count = count_ref[unit]
        q = q_ref[unit]

        def step(t, state):
            top, total, acc = state
            rows = [pl.multiple_of(list_ref[unit, 4 * t + i] * BLOCK, BLOCK) for i in range(4)]
            keys = jnp.concatenate([k_flat[pl.ds(r, BLOCK), :] for r in rows], axis=0)
            values = jnp.concatenate([v_flat[pl.ds(r, BLOCK), :] for r in rows], axis=0)
            s = dot_t(q, keys)
            s = jnp.where(col < (count - 4 * t) * BLOCK, s, FLOOR)
            new_top = jnp.maximum(top, jnp.max(s, axis=1, keepdims=True))
            p = jnp.exp2((s - new_top) * SCALE)
            alpha = jnp.exp2((top - new_top) * SCALE)
            total = total * alpha + jnp.sum(p, axis=1, keepdims=True)
            acc = acc * alpha + jnp.dot(
                p.astype(jnp.bfloat16), values, preferred_element_type=jnp.float32
            )
            return new_top, total, acc

        top, total, acc = lax.fori_loop(
            0,
            lax.div(count + 3, 4),
            step,
            (
                jnp.full((BLOCK, 1), FLOOR, jnp.float32),
                jnp.zeros((BLOCK, 1), jnp.float32),
                jnp.zeros((BLOCK, HEAD), jnp.float32),
            ),
        )
        sb, row = place(unit)
        out_ref[sb, pl.ds(row, BLOCK), :] = (acc / total).astype(jnp.bfloat16)
        return carry

    def shared_unit(unit, carry):
        count = shared_count_ref[unit]
        q = q_ref[12 + unit]
        rows = []
        for i in range(16):
            block = shared_list_ref[unit, i]
            sb = lax.div(block, 3)
            for e in range(2):
                h = (block - 3 * sb) * 8 + group + 4 * e
                chunk = lax.div(h, 6)
                slot = lax.div(h - 6 * chunk, 4)
                rows.append(pl.multiple_of((sb * CHUNKS + chunk) * EXT + slot * HALF, HALF))
        keys = jnp.concatenate([ke_flat[pl.ds(r, HALF), :] for r in rows], axis=0)
        values = jnp.concatenate([ve_flat[pl.ds(r, HALF), :] for r in rows], axis=0)
        s = dot_t(q, keys)
        s = jnp.where(col < count * (2 * HALF), s, FLOOR)
        top = jnp.max(s, axis=1, keepdims=True)
        p = jnp.exp2((s - top) * SCALE)
        total = jnp.sum(p, axis=1, keepdims=True)
        acc = jnp.dot(p.astype(jnp.bfloat16), values, preferred_element_type=jnp.float32)
        sb, row = place(unit)
        out_ref[sb, pl.ds(SUPER + row, BLOCK), :] = (acc / total).astype(jnp.bfloat16)
        level = top * SCALE + jnp.log2(total)
        level = jnp.sum(jnp.where(eye, level, 0.0), axis=0, keepdims=True)
        high = level.astype(jnp.bfloat16).astype(jnp.float32)
        rest = level - high
        mid = rest.astype(jnp.bfloat16).astype(jnp.float32)
        low = rest - mid
        index = lax.broadcasted_iota(jnp.int32, (STATS, HEAD), 0)
        tile = jnp.where(index == 0, high, jnp.where(index == 1, mid, jnp.where(index == 2, low, 0.0)))
        at = pl.multiple_of(2 * SUPER + (unit - 3 * sb) * STATS, STATS)
        out_ref[sb, pl.ds(at, STATS), :] = tile.astype(jnp.bfloat16)
        return carry

    lax.fori_loop(0, 12, main_unit, 0)
    lax.fori_loop(0, 12, shared_unit, 0)


def attention(where, lists, counts, shared_lists, shared_counts, q, pieces):
    smem = pl.BlockSpec(memory_space=pltpu.SMEM)
    vmem = pl.BlockSpec(memory_space=pltpu.VMEM)
    hbm = pl.BlockSpec(memory_space=pl.ANY)
    return pl.pallas_call(
        attention_kernel,
        out_shape=jax.ShapeDtypeStruct((4, 2 * SUPER + 3 * STATS, HEAD), jnp.bfloat16),
        in_specs=[smem] * 5 + [vmem] + [hbm] * 10,
        out_specs=vmem,
        scratch_shapes=[
            pltpu.VMEM((4, 2, 4, CHUNKS, ROWS, HEAD), jnp.bfloat16),
            pltpu.VMEM((4, 2, 4, CHUNKS, ROWS, HEAD), jnp.bfloat16),
            pltpu.VMEM((4, 2, 4, CHUNKS, EXT, HEAD), jnp.bfloat16),
            pltpu.VMEM((4, 2, 4, CHUNKS, EXT, HEAD), jnp.bfloat16),
            pltpu.SemaphoreType.DMA((32,)),
        ],
        compiler_params=pltpu.CompilerParams(vmem_limit_bytes=40 * 1024 * 1024),
        cost_estimate=pl.CostEstimate(
            flops=4 * 240 * BLOCK * BLOCK * HEAD, bytes_accessed=10_000_000, transcendentals=4_000_000
        ),
    )(where, lists, counts, shared_lists, shared_counts, q, *pieces)


def to_groups(main):
    rows = main.shape[0]
    return main.transpose(2, 1, 0, 3).reshape(16, rows, HEAD)


def shared_keys(rows, core):
    runs = jnp.pad(rows, ((0, 32), (0, 0), (0, 0))).reshape(2, 4, HALF, 4, HEAD)
    runs = jnp.where(core == 0, runs, jnp.roll(runs, 2, axis=1))
    return runs.transpose(1, 3, 0, 2, 4).reshape(16, EXT, HEAD)


def per_device(queries, key_rows, value_rows, block_list, block_count, w_out):
    xh, zh, zl, y, xl, c = [lax.axis_index(name) for name in NAMES]
    u = 2 * xl + c
    group = 2 * xh + zh
    k5 = key_rows.reshape(ROWS, 4, 5, HEAD)
    v5 = value_rows.reshape(ROWS, 4, 5, HEAD)
    q5 = queries.reshape(ROWS, 4, 5, HEAD)
    kv = jnp.concatenate(
        [
            to_groups(k5[:, :, :4]),
            to_groups(v5[:, :, :4]),
            shared_keys(k5[:, :, 4], c),
            shared_keys(v5[:, :, 4], c),
        ],
        axis=1,
    )
    kv = lax.all_to_all(kv, SPREAD, 0, 0, tiled=True).reshape(4, CHUNKS, 2 * ROWS + 2 * EXT, HEAD)

    q_shared = jnp.broadcast_to(q5[:, :, 4:], (ROWS, 4, 4, HEAD))
    q = jnp.stack([to_groups(q5[:, :, :4]), to_groups(q_shared)], axis=1)
    q = lax.all_to_all(q, SPREAD, 0, 0, tiled=True)
    q = q.reshape(4, CHUNKS, 2, ROWS, HEAD).transpose(2, 0, 1, 3, 4).reshape(24, BLOCK, HEAD)

    a01, am0, ap0 = swap(kv), ring_up(kv), ring_down(kv)
    a11, am1, a20 = swap(ap0), ring_up(a01), ring_down(ap0)
    last_k = swap(a20[:, :, :ROWS])
    last_v = ring_up(am1[:, :, ROWS : 2 * ROWS])
    last_e = ring_down(a11[:, :, 2 * ROWS :])
    pieces = (kv, a01, am0, ap0, a11, am1, a20, last_k, last_v, last_e)

    def pick(table, head):
        mine = lax.dynamic_index_in_dim(table, head, 0, keepdims=False)
        mine = mine.reshape((4, 8, 3) + mine.shape[1:])
        return lax.dynamic_index_in_dim(mine, 4 * zl + y, 1, keepdims=False)

    lists = pick(block_list, 5 * u + group).reshape(12, 16)
    counts = pick(block_count, 5 * u + group).reshape(12)
    shared_lists = pick(block_list, 5 * u + 4).reshape(12, 16)
    shared_counts = pick(block_count, 5 * u + 4).reshape(12)
    where = jnp.stack([y, zl, group]).astype(jnp.int32)

    out = attention(where, lists, counts, shared_lists, shared_counts, q, pieces)
    out = lax.all_to_all(out, ("xh", "zh"), 0, 0, tiled=True)

    heads = out[:, :SUPER]
    shares = out[:, SUPER : 2 * SUPER].astype(jnp.float32)
    level = out[:, 2 * SUPER :].reshape(4, 3, STATS, BLOCK)[:, :, :3].astype(jnp.float32)
    level = jnp.sum(level, axis=2).reshape(4, SUPER, 1)
    weight = jnp.exp2(level - jnp.max(level, axis=0, keepdims=True))
    shared = jnp.sum(shares * weight, axis=0) / jnp.sum(weight, axis=0)
    attended = jnp.concatenate(
        [heads.transpose(1, 0, 2).reshape(SUPER, 4 * HEAD), shared.astype(jnp.bfloat16)], axis=1
    )
    return lax.psum_scatter(
        jnp.dot(attended, w_out, preferred_element_type=jnp.float32).astype(jnp.bfloat16),
        ("xl", "c"),
        scatter_dimension=0,
        tiled=True,
    )


def solution(mesh):
    fine = Mesh(mesh.devices.reshape(SIZES), GRID)
    rows = P(NAMES, None)
    return jax.shard_map(
        per_device,
        mesh=fine,
        in_specs=(rows, rows, rows, P(), P(), P(("xl", "c"), None)),
        out_specs=rows,
        check_vma=False,
    )
```

```python
import functools

import jax
import jax.numpy as jnp
from jax import lax
from jax.experimental import pallas as pl
from jax.experimental.pallas import tpu as pltpu
from jax.sharding import Mesh, PartitionSpec as P

HEAD = 128
BLOCK = 128
ROWS = 96
CHUNKS = 4
SUPER = ROWS * CHUNKS
EXT = 32
HALF = 16
KV = 2 * ROWS + 2 * EXT
LOG2E = 1.4426950408889634
SCALE = HEAD ** -0.5 * LOG2E
FLOOR = -1e30
NAMES = ("xh", "zh", "zl", "y", "xl", "c")
GRID = ("xl", "c", "xh", "zh", "zl", "y")
SIZES = (2, 2, 2, 2, 2, 4)
SPREAD = ("xh", "zh", "xl", "c")
STATS = 16
UNITS = 12
SLOTS = 16
SMEM = pl.BlockSpec(memory_space=pltpu.SMEM)
VMEM = pl.BlockSpec(memory_space=pltpu.VMEM)
HBM = pl.BlockSpec(memory_space=pl.ANY)


def ring_up(x):
    return lax.ppermute(x, "y", [(i, (i + 1) % 4) for i in range(4)])


def ring_down(x):
    return lax.ppermute(x, "y", [(i, (i - 1) % 4) for i in range(4)])


def swap(x):
    return lax.ppermute(x, "zl", [(0, 1), (1, 0)])


def plan_kernel(where_ref, count_ref, table_ref, main_ref, ext0_ref, ext1_ref, n_ref, lists, sem):
    y, zl, head, shared, group = [where_ref[i] for i in range(5)]
    copies = [
        pltpu.make_async_copy(table_ref.at[h], lists.at[i], sem.at[i])
        for i, h in enumerate((head, shared))
    ]
    for copy in copies:
        copy.start()
    for copy in copies:
        copy.wait()

    def unit_step(unit, carry):
        which = lax.div(unit, UNITS)
        local = unit - which * UNITS
        sb = lax.div(local, 3)
        row = (sb * 8 + zl * 4 + y) * 3 + (local - 3 * sb)
        count = count_ref[jnp.where(which == 0, head, shared), row]
        for stage in range(3):
            n_ref[stage, unit] = 0

        def slot_step(slot, carry):
            block = lists[which, row, slot]
            sb = lax.div(block, 3)
            r = block - 3 * sb
            column = lax.div(sb, 8)
            zy = sb - 8 * column
            dz = lax.rem(lax.div(zy, 4) + zl, 2)
            dy = lax.rem(lax.rem(zy, 4) + 4 - y, 4)
            stage = jnp.where(
                dz == 0, jnp.where(dy == 2, 1, 0), jnp.where(dy == 0, 0, jnp.where(dy == 2, 2, 1))
            )
            piece = jnp.where(
                dz == 0,
                jnp.where(dy == 0, 0, jnp.where(dy == 3, 2, jnp.where(dy == 1, 3, 2))),
                jnp.where(dy == 0, 1, jnp.where(dy == 3, 1, 0)),
            )
            n = n_ref[stage, unit]
            n_ref[stage, unit] = n + 1
            place = piece * 4 + column
            main_ref[stage * 24 + unit, n] = (place * 3 + r) * BLOCK
            for e, ref in enumerate((ext0_ref, ext1_ref)):
                h = r * 8 + group + 4 * e
                chunk = lax.div(h, 6)
                run = lax.div(h - 6 * chunk, 4)
                ref[stage * 24 + unit, n] = (place * CHUNKS + chunk) * EXT + run * HALF
            return carry

        lax.fori_loop(0, count, slot_step, 0)
        return carry

    lax.fori_loop(0, 2 * UNITS, unit_step, 0)


def plan(where, counts, table):
    lists = jax.ShapeDtypeStruct((72, SLOTS), jnp.int32)
    return pl.pallas_call(
        plan_kernel,
        out_shape=(lists, lists, lists, jax.ShapeDtypeStruct((3, 2 * UNITS), jnp.int32)),
        in_specs=[SMEM, SMEM, HBM],
        out_specs=(SMEM, SMEM, SMEM, SMEM),
        scratch_shapes=[pltpu.SMEM((2, 96, SLOTS), jnp.int32), pltpu.SemaphoreType.DMA((2,))],
        cost_estimate=pl.CostEstimate(flops=8_000_000_000, bytes_accessed=100_000, transcendentals=0),
    )(where, counts, table)


def stage_kernel(stage, shapes, *refs):
    first, last = stage == 0, stage == 2
    main_ref, ext0_ref, ext1_ref, n_ref, q_ref = refs[:5]
    refs = refs[5:]
    if not first:
        acc_in, ml_in = refs[:2]
        refs = refs[2:]
    sources, refs = refs[: len(shapes)], refs[len(shapes) :]
    if last:
        out_ref = refs[0]
        refs = refs[1:]
    else:
        acc_out, ml_out = refs[:2]
        refs = refs[2:]
    k_main, v_main, k_ext, v_ext, sem = refs
    copies = []
    for source, parts in zip(sources, shapes):
        lo = 0
        for piece, name in parts:
            target = {"k": k_main, "v": v_main, "a": k_ext, "b": v_ext}[name]
            rows = ROWS if name in "kv" else EXT
            copy = pltpu.make_async_copy(
                source.at[:, :, pl.ds(lo, rows)], target.at[piece], sem.at[len(copies)]
            )
            copy.start()
            copies.append(copy)
            lo += rows
    for copy in copies:
        copy.wait()

    pieces = k_main.shape[0]
    k_flat = k_main.reshape(pieces * 4 * SUPER, HEAD)
    v_flat = v_main.reshape(pieces * 4 * SUPER, HEAD)
    ke_flat = k_ext.reshape(pieces * 4 * CHUNKS * EXT, HEAD)
    ve_flat = v_ext.reshape(pieces * 4 * CHUNKS * EXT, HEAD)
    lane = lax.broadcasted_iota(jnp.int32, (BLOCK, HEAD), 1)
    eye = lax.broadcasted_iota(jnp.int32, (BLOCK, BLOCK), 0) == lane

    def dot_t(a, b):
        return lax.dot_general(a, b, (((1,), (1,)), ((), ())), preferred_element_type=jnp.float32)

    def update(q, keys, values, live, state):
        top, total, acc = state
        s = dot_t(q, keys)
        col = lax.broadcasted_iota(jnp.int32, s.shape, 1)
        s = jnp.where(col < live, s, FLOOR)
        new_top = jnp.maximum(top, jnp.max(s, axis=1, keepdims=True))
        p = jnp.exp2((s - new_top) * SCALE)
        alpha = jnp.exp2((top - new_top) * SCALE)
        total = total * alpha + jnp.sum(p, axis=1, keepdims=True)
        acc = acc * alpha + jnp.dot(p.astype(jnp.bfloat16), values, preferred_element_type=jnp.float32)
        return new_top, total, acc

    def begin(unit):
        if first:
            return (
                jnp.full((BLOCK, 1), FLOOR, jnp.float32),
                jnp.zeros((BLOCK, 1), jnp.float32),
                jnp.zeros((BLOCK, HEAD), jnp.float32),
            )
        ml = ml_in[unit]
        return ml[:, :1], ml[:, HEAD // 2 : HEAD // 2 + 1], acc_in[unit]

    def keep(unit, state):
        top, total, acc = state
        acc_out[unit] = acc
        ml_out[unit] = jnp.where(lane < HEAD // 2, top, total)

    def run(unit, group, width, rows_of, key_flat, value_flat, rows):
        n = n_ref[stage, unit]
        q = q_ref[unit]

        def step(t, state):
            starts = []
            for i in range(group):
                starts += rows_of(stage * 24 + unit, jnp.minimum(group * t + i, n - 1))
            keys = jnp.concatenate([key_flat[pl.ds(r, rows), :] for r in starts], axis=0)
            values = jnp.concatenate([value_flat[pl.ds(r, rows), :] for r in starts], axis=0)
            return update(q, keys, values, (n - group * t) * width, state)

        return lax.fori_loop(0, lax.div(n + (group - 1), group), step, begin(unit))

    def main_rows(row, slot):
        return [pl.multiple_of(main_ref[row, slot], BLOCK)]

    def ext_rows(row, slot):
        return [pl.multiple_of(ref[row, slot], HALF) for ref in (ext0_ref, ext1_ref)]

    def main_unit(unit, carry):
        state = run(unit, 2 if last else 4, BLOCK, main_rows, k_flat, v_flat, BLOCK)
        if not last:
            keep(unit, state)
            return carry
        top, total, acc = state
        sb = lax.div(unit, 3)
        row = pl.multiple_of((unit - 3 * sb) * BLOCK, BLOCK)
        out_ref[sb, pl.ds(row, BLOCK), :] = (acc / total).astype(jnp.bfloat16)
        return carry

    def ext_unit(local, carry):
        unit = UNITS + local
        state = run(unit, 4 if last else 8, 2 * HALF, ext_rows, ke_flat, ve_flat, HALF)
        if not last:
            keep(unit, state)
            return carry
        top, total, acc = state
        sb = lax.div(local, 3)
        row = pl.multiple_of((local - 3 * sb) * BLOCK, BLOCK)
        out_ref[sb, pl.ds(SUPER + row, BLOCK), :] = (acc / total).astype(jnp.bfloat16)
        level = top * SCALE + jnp.log2(total)
        level = jnp.sum(jnp.where(eye, level, 0.0), axis=0, keepdims=True)
        high = level.astype(jnp.bfloat16).astype(jnp.float32)
        rest = level - high
        mid = rest.astype(jnp.bfloat16).astype(jnp.float32)
        low = rest - mid
        index = lax.broadcasted_iota(jnp.int32, (STATS, HEAD), 0)
        tile = jnp.where(index == 0, high, jnp.where(index == 1, mid, jnp.where(index == 2, low, 0.0)))
        at = pl.multiple_of(2 * SUPER + (local - 3 * sb) * STATS, STATS)
        out_ref[sb, pl.ds(at, STATS), :] = tile.astype(jnp.bfloat16)
        return carry

    lax.fori_loop(0, UNITS, main_unit, 0)
    lax.fori_loop(0, UNITS, ext_unit, 0)


def attend(stage, plans, q, state, sources, shapes):
    pieces = 1 + max(piece for parts in shapes for piece, _ in parts)
    copies = sum(len(parts) for parts in shapes)
    kept = jax.ShapeDtypeStruct((2 * UNITS, BLOCK, HEAD), jnp.float32)
    if stage == 2:
        out_shape = jax.ShapeDtypeStruct((4, 2 * SUPER + 3 * STATS, HEAD), jnp.bfloat16)
        out_specs = VMEM
    else:
        out_shape, out_specs = (kept, kept), (VMEM, VMEM)
    share = pieces / 8
    return pl.pallas_call(
        functools.partial(stage_kernel, stage, shapes),
        out_shape=out_shape,
        in_specs=[SMEM] * 4 + [VMEM] * (1 + len(state)) + [HBM] * len(sources),
        out_specs=out_specs,
        scratch_shapes=[
            pltpu.VMEM((pieces, 4, CHUNKS, ROWS, HEAD), jnp.bfloat16),
            pltpu.VMEM((pieces, 4, CHUNKS, ROWS, HEAD), jnp.bfloat16),
            pltpu.VMEM((pieces, 4, CHUNKS, EXT, HEAD), jnp.bfloat16),
            pltpu.VMEM((pieces, 4, CHUNKS, EXT, HEAD), jnp.bfloat16),
            pltpu.SemaphoreType.DMA((copies,)),
        ],
        compiler_params=pltpu.CompilerParams(vmem_limit_bytes=32 * 1024 * 1024),
        cost_estimate=pl.CostEstimate(
            flops=int(share * 20e9), bytes_accessed=int(share * 10e6), transcendentals=int(share * 4e6)
        ),
    )(*plans, q, *state, *sources)


def to_groups(main):
    rows = main.shape[0]
    return main.transpose(2, 1, 0, 3).reshape(16, rows, HEAD)


def shared_keys(rows, core):
    runs = jnp.pad(rows, ((0, 32), (0, 0), (0, 0))).reshape(2, 4, HALF, 4, HEAD)
    runs = jnp.where(core == 0, runs, jnp.roll(runs, 2, axis=1))
    return runs.transpose(1, 3, 0, 2, 4).reshape(16, EXT, HEAD)


def per_device(queries, key_rows, value_rows, block_list, block_count, w_out):
    xh, zh, zl, y, xl, c = [lax.axis_index(name) for name in NAMES]
    u = 2 * xl + c
    group = 2 * xh + zh
    k5 = key_rows.reshape(ROWS, 4, 5, HEAD)
    v5 = value_rows.reshape(ROWS, 4, 5, HEAD)
    q5 = queries.reshape(ROWS, 4, 5, HEAD)
    sent = jnp.concatenate(
        [
            to_groups(k5[:, :, :4]),
            to_groups(v5[:, :, :4]),
            shared_keys(k5[:, :, 4], c),
            shared_keys(v5[:, :, 4], c),
            to_groups(q5[:, :, :4]),
            to_groups(jnp.broadcast_to(q5[:, :, 4:], (ROWS, 4, 4, HEAD))),
        ],
        axis=1,
    )
    got = lax.all_to_all(sent, SPREAD, 0, 0, tiled=True).reshape(4, CHUNKS, KV + 2 * ROWS, HEAD)
    kv = got[:, :, :KV]

    where = jnp.stack([y, zl, 5 * u + group, 5 * u + 4, group]).astype(jnp.int32)
    plans = plan(where, block_count, block_list)
    q = got[:, :, KV:].reshape(4, CHUNKS, 2, ROWS, HEAD)
    q = q.transpose(2, 0, 1, 3, 4).reshape(2 * UNITS, BLOCK, HEAD)

    a01, am0, ap0 = swap(kv), ring_up(kv), ring_down(kv)
    a01, am0, ap0, q, plans = lax.optimization_barrier((a01, am0, ap0, q, plans))
    a11, am1, a20 = swap(ap0), ring_up(a01), ring_down(ap0)
    whole = lambda piece: tuple((piece, name) for name in "kvab")
    state = attend(0, plans, q, (), (kv, a01, am0, ap0), tuple(whole(i) for i in range(4)))
    a11, am1, a20, state = lax.optimization_barrier((a11, am1, a20, state))
    last_k = swap(a20[:, :, :ROWS])
    last_v = ring_up(am1[:, :, ROWS : 2 * ROWS])
    last_e = ring_down(a11[:, :, 2 * ROWS :])
    state = attend(1, plans, q, state, (a11, am1, a20), tuple(whole(i) for i in range(3)))
    out = attend(
        2, plans, q, state, (last_k, last_v, last_e), (((0, "k"),), ((0, "v"),), ((0, "a"), (0, "b")))
    )
    out = lax.all_to_all(out, ("xh", "zh"), 0, 0, tiled=True)

    heads = out[:, :SUPER]
    shares = out[:, SUPER : 2 * SUPER].astype(jnp.float32)
    level = out[:, 2 * SUPER :].reshape(4, 3, STATS, BLOCK)[:, :, :3].astype(jnp.float32)
    level = jnp.sum(level, axis=2).reshape(4, SUPER, 1)
    weight = jnp.exp2(level - jnp.max(level, axis=0, keepdims=True))
    shared = jnp.sum(shares * weight, axis=0) / jnp.sum(weight, axis=0)
    attended = jnp.concatenate(
        [heads.transpose(1, 0, 2).reshape(SUPER, 4 * HEAD), shared.astype(jnp.bfloat16)], axis=1
    )
    return lax.psum_scatter(
        jnp.dot(attended, w_out, preferred_element_type=jnp.float32).astype(jnp.bfloat16),
        ("xl", "c"),
        scatter_dimension=0,
        tiled=True,
    )


def solution(mesh):
    fine = Mesh(mesh.devices.reshape(SIZES), GRID)
    rows = P(NAMES, None)
    return jax.shard_map(
        per_device,
        mesh=fine,
        in_specs=(rows, rows, rows, P(), P(), P(("xl", "c"), None)),
        out_specs=rows,
        check_vma=False,
    )
```

```python
import functools

import jax
import jax.numpy as jnp
from jax import lax
from jax.experimental import pallas as pl
from jax.experimental.pallas import tpu as pltpu
from jax.sharding import Mesh, PartitionSpec as P

HEAD = 128
BLOCK = 128
ROWS = 96
CHUNKS = 4
SUPER = ROWS * CHUNKS
EXT = 32
HALF = 16
KV = 2 * ROWS + 2 * EXT
LOG2E = 1.4426950408889634
SCALE = HEAD ** -0.5 * LOG2E
FLOOR = -1e30
NAMES = ("xh", "zh", "zl", "y", "xl", "c")
GRID = ("xl", "c", "xh", "zh", "zl", "y")
SIZES = (2, 2, 2, 2, 2, 4)
SPREAD = ("xh", "zh", "xl", "c")
STATS = 16
UNITS = 12
SLOTS = 16
MAIN_UNROLL = (12, 12, 12)
MAIN_GROUP = (2, 2, 2)
EXT_UNROLL = (12, 12, 12)
EXT_GROUP = (4, 4, 4)
SMEM = pl.BlockSpec(memory_space=pltpu.SMEM)
VMEM = pl.BlockSpec(memory_space=pltpu.VMEM)
HBM = pl.BlockSpec(memory_space=pl.ANY)


def ring_up(x):
    return lax.ppermute(x, "y", [(i, (i + 1) % 4) for i in range(4)])


def ring_down(x):
    return lax.ppermute(x, "y", [(i, (i - 1) % 4) for i in range(4)])


def swap(x):
    return lax.ppermute(x, "zl", [(0, 1), (1, 0)])


def plan_kernel(where_ref, count_ref, table_ref, main_ref, ext0_ref, ext1_ref, n_ref, lists, sem):
    y, zl, head, shared, group = [where_ref[i] for i in range(5)]
    copies = [
        pltpu.make_async_copy(table_ref.at[h], lists.at[i], sem.at[i])
        for i, h in enumerate((head, shared))
    ]
    for copy in copies:
        copy.start()
    for copy in copies:
        copy.wait()

    def unit_step(unit, carry):
        which = lax.div(unit, UNITS)
        local = unit - which * UNITS
        sb = lax.div(local, 3)
        row = (sb * 8 + zl * 4 + y) * 3 + (local - 3 * sb)
        count = count_ref[jnp.where(which == 0, head, shared), row]
        for stage in range(3):
            n_ref[stage, unit] = 0
            for ref in (main_ref, ext0_ref, ext1_ref):
                ref[stage * 24 + unit, 0] = 0

        def slot_step(slot, carry):
            block = lists[which, row, slot]
            sb = lax.div(block, 3)
            r = block - 3 * sb
            column = lax.div(sb, 8)
            zy = sb - 8 * column
            dz = lax.rem(lax.div(zy, 4) + zl, 2)
            dy = lax.rem(lax.rem(zy, 4) + 4 - y, 4)
            stage = jnp.where(
                dz == 0, jnp.where(dy == 2, 1, 0), jnp.where(dy == 0, 0, jnp.where(dy == 2, 2, 1))
            )
            piece = jnp.where(
                dz == 0,
                jnp.where(dy == 0, 0, jnp.where(dy == 3, 2, jnp.where(dy == 1, 3, 2))),
                jnp.where(dy == 0, 1, jnp.where(dy == 3, 1, 0)),
            )
            n = n_ref[stage, unit]
            n_ref[stage, unit] = n + 1
            place = piece * 4 + column
            main_ref[stage * 24 + unit, n] = (place * 3 + r) * BLOCK
            for e, ref in enumerate((ext0_ref, ext1_ref)):
                h = r * 8 + group + 4 * e
                chunk = lax.div(h, 6)
                run = lax.div(h - 6 * chunk, 4)
                ref[stage * 24 + unit, n] = (place * CHUNKS + chunk) * EXT + run * HALF
            return carry

        lax.fori_loop(0, count, slot_step, 0)
        return carry

    lax.fori_loop(0, 2 * UNITS, unit_step, 0)


def plan(where, counts, table):
    lists = jax.ShapeDtypeStruct((72, SLOTS), jnp.int32)
    return pl.pallas_call(
        plan_kernel,
        out_shape=(lists, lists, lists, jax.ShapeDtypeStruct((3, 2 * UNITS), jnp.int32)),
        in_specs=[SMEM, SMEM, HBM],
        out_specs=(SMEM, SMEM, SMEM, SMEM),
        scratch_shapes=[pltpu.SMEM((2, 96, SLOTS), jnp.int32), pltpu.SemaphoreType.DMA((2,))],
        cost_estimate=pl.CostEstimate(flops=8_000_000_000, bytes_accessed=100_000, transcendentals=0),
    )(where, counts, table)


def stage_kernel(stage, shapes, *refs):
    first, last = stage == 0, stage == 2
    main_ref, ext0_ref, ext1_ref, n_ref, q_ref = refs[:5]
    refs = refs[5:]
    if not first:
        before = refs[:3]
        refs = refs[3:]
    sources, refs = refs[: len(shapes)], refs[len(shapes) :]
    if last:
        out_ref = refs[0]
        refs = refs[1:]
        k_main, v_main, k_ext, v_ext, sem, top_ref, tot_ref, acc_ref = refs
    else:
        top_ref, tot_ref, acc_ref, k_main, v_main, k_ext, v_ext, sem = refs
    copies = []
    for source, parts in zip(sources, shapes):
        lo = 0
        for piece, name in parts:
            target = {"k": k_main, "v": v_main, "a": k_ext, "b": v_ext}[name]
            rows = ROWS if name in "kv" else EXT
            copy = pltpu.make_async_copy(
                source.at[:, :, pl.ds(lo, rows)], target.at[piece], sem.at[len(copies)]
            )
            copy.start()
            copies.append(copy)
            lo += rows

    def begin(unit, carry):
        if first:
            top_ref[unit] = jnp.full((BLOCK, HEAD), FLOOR, jnp.float32)
            tot_ref[unit] = jnp.zeros((BLOCK, HEAD), jnp.float32)
            acc_ref[unit] = jnp.zeros((BLOCK, HEAD), jnp.float32)
        else:
            for old, new in zip(before, (top_ref, tot_ref, acc_ref)):
                new[unit] = old[unit]
        return carry

    lax.fori_loop(0, 2 * UNITS, begin, 0)
    for copy in copies:
        copy.wait()

    pieces = k_main.shape[0]
    k_flat = k_main.reshape(pieces * 4 * SUPER, HEAD)
    v_flat = v_main.reshape(pieces * 4 * SUPER, HEAD)
    ke_flat = k_ext.reshape(pieces * 4 * CHUNKS * EXT, HEAD)
    ve_flat = v_ext.reshape(pieces * 4 * CHUNKS * EXT, HEAD)
    lane = lax.broadcasted_iota(jnp.int32, (BLOCK, HEAD), 1)
    eye = lax.broadcasted_iota(jnp.int32, (BLOCK, BLOCK), 0) == lane

    def dot_t(a, b):
        return lax.dot_general(a, b, (((1,), (1,)), ((), ())), preferred_element_type=jnp.float32)

    def main_rows(row, slot):
        return [pl.multiple_of(main_ref[row, slot], BLOCK)]

    def ext_rows(row, slot):
        return [pl.multiple_of(ref[row, slot], HALF) for ref in (ext0_ref, ext1_ref)]

    def run(units, group, rows_of, key_flat, value_flat, rows):
        width = len(rows_of(0, 0)) * rows
        ns = [n_ref[stage, unit] for unit in units]
        most = functools.reduce(jnp.maximum, ns)

        def step(t, carry):
            col = lax.broadcasted_iota(jnp.int32, (BLOCK, group * width), 1)
            values, scores = [], []
            for unit, n in zip(units, ns):
                starts = []
                for i in range(group):
                    slot = jnp.maximum(jnp.minimum(group * t + i, n - 1), 0)
                    starts += rows_of(stage * 24 + unit, slot)
                keys = jnp.concatenate([key_flat[pl.ds(r, rows), :] for r in starts], axis=0)
                values.append(
                    jnp.concatenate([value_flat[pl.ds(r, rows), :] for r in starts], axis=0)
                )
                s = dot_t(q_ref[unit], keys)
                scores.append(jnp.where(col < (n - group * t) * width, s, 2 * FLOOR))
            for unit, s, v in zip(units, scores, values):
                top = top_ref[unit][:, :1]
                new_top = jnp.maximum(top, jnp.max(s, axis=1, keepdims=True))
                p = jnp.exp2((s - new_top) * SCALE)
                alpha = jnp.exp2((top - new_top) * SCALE)
                part = functools.reduce(
                    jnp.add, [p[:, i : i + HEAD] for i in range(0, group * width, HEAD)]
                )
                product = jnp.dot(p.astype(jnp.bfloat16), v, preferred_element_type=jnp.float32)
                top_ref[unit] = jnp.broadcast_to(new_top, (BLOCK, HEAD))
                tot_ref[unit] = tot_ref[unit] * alpha + part
                acc_ref[unit] = acc_ref[unit] * alpha + product
            return carry

        lax.fori_loop(0, lax.div(most + (group - 1), group), step, 0)

    def finish(unit):
        total = jnp.sum(tot_ref[unit], axis=1, keepdims=True)
        return top_ref[unit][:, :1], total, (acc_ref[unit] / total).astype(jnp.bfloat16)

    def main_units(index, carry):
        units = [index * MAIN_UNROLL[stage] + i for i in range(MAIN_UNROLL[stage])]
        run(units, MAIN_GROUP[stage], main_rows, k_flat, v_flat, BLOCK)
        if last:
            for unit in units:
                sb = lax.div(unit, 3)
                row = pl.multiple_of((unit - 3 * sb) * BLOCK, BLOCK)
                out_ref[sb, pl.ds(row, BLOCK), :] = finish(unit)[2]
        return carry

    def ext_units(index, carry):
        locals_ = [index * EXT_UNROLL[stage] + i for i in range(EXT_UNROLL[stage])]
        run([UNITS + i for i in locals_], EXT_GROUP[stage], ext_rows, ke_flat, ve_flat, HALF)
        if last:
            for local in locals_:
                top, total, value = finish(UNITS + local)
                sb = lax.div(local, 3)
                row = pl.multiple_of((local - 3 * sb) * BLOCK, BLOCK)
                out_ref[sb, pl.ds(SUPER + row, BLOCK), :] = value
                level = top * SCALE + jnp.log2(total)
                level = jnp.sum(jnp.where(eye, level, 0.0), axis=0, keepdims=True)
                high = level.astype(jnp.bfloat16).astype(jnp.float32)
                rest = level - high
                mid = rest.astype(jnp.bfloat16).astype(jnp.float32)
                low = rest - mid
                index_ = lax.broadcasted_iota(jnp.int32, (STATS, HEAD), 0)
                tile = jnp.where(
                    index_ == 0, high, jnp.where(index_ == 1, mid, jnp.where(index_ == 2, low, 0.0))
                )
                at = pl.multiple_of(2 * SUPER + (local - 3 * sb) * STATS, STATS)
                out_ref[sb, pl.ds(at, STATS), :] = tile.astype(jnp.bfloat16)
        return carry

    lax.fori_loop(0, UNITS // MAIN_UNROLL[stage], main_units, 0)
    lax.fori_loop(0, UNITS // EXT_UNROLL[stage], ext_units, 0)


def attend(stage, plans, q, state, sources, shapes):
    pieces = 1 + max(piece for parts in shapes for piece, _ in parts)
    copies = sum(len(parts) for parts in shapes)
    kept = jax.ShapeDtypeStruct((2 * UNITS, BLOCK, HEAD), jnp.float32)
    scratch = [
        pltpu.VMEM((pieces, 4, CHUNKS, ROWS, HEAD), jnp.bfloat16),
        pltpu.VMEM((pieces, 4, CHUNKS, ROWS, HEAD), jnp.bfloat16),
        pltpu.VMEM((pieces, 4, CHUNKS, EXT, HEAD), jnp.bfloat16),
        pltpu.VMEM((pieces, 4, CHUNKS, EXT, HEAD), jnp.bfloat16),
        pltpu.SemaphoreType.DMA((copies,)),
    ]
    if stage == 2:
        out_shape = jax.ShapeDtypeStruct((4, 2 * SUPER + 3 * STATS, HEAD), jnp.bfloat16)
        out_specs = VMEM
        scratch += [pltpu.VMEM(kept.shape, kept.dtype)] * 3
    else:
        out_shape, out_specs = (kept,) * 3, (VMEM,) * 3
    share = pieces / 8
    return pl.pallas_call(
        functools.partial(stage_kernel, stage, shapes),
        out_shape=out_shape,
        in_specs=[SMEM] * 4 + [VMEM] * (1 + len(state)) + [HBM] * len(sources),
        out_specs=out_specs,
        scratch_shapes=scratch,
        compiler_params=pltpu.CompilerParams(vmem_limit_bytes=32 * 1024 * 1024),
        cost_estimate=pl.CostEstimate(
            flops=int(share * 20e9), bytes_accessed=int(share * 10e6), transcendentals=int(share * 4e6)
        ),
    )(*plans, q, *state, *sources)


def to_groups(main):
    rows = main.shape[0]
    return main.transpose(2, 1, 0, 3).reshape(16, rows, HEAD)


def shared_keys(rows, core):
    runs = jnp.pad(rows, ((0, 32), (0, 0), (0, 0))).reshape(2, 4, HALF, 4, HEAD)
    runs = jnp.where(core == 0, runs, jnp.roll(runs, 2, axis=1))
    return runs.transpose(1, 3, 0, 2, 4).reshape(16, EXT, HEAD)


def per_device(queries, key_rows, value_rows, block_list, block_count, w_out):
    xh, zh, zl, y, xl, c = [lax.axis_index(name) for name in NAMES]
    u = 2 * xl + c
    group = 2 * xh + zh
    k5 = key_rows.reshape(ROWS, 4, 5, HEAD)
    v5 = value_rows.reshape(ROWS, 4, 5, HEAD)
    q5 = queries.reshape(ROWS, 4, 5, HEAD)
    sent = jnp.concatenate(
        [
            to_groups(k5[:, :, :4]),
            to_groups(v5[:, :, :4]),
            shared_keys(k5[:, :, 4], c),
            shared_keys(v5[:, :, 4], c),
            to_groups(q5[:, :, :4]),
            to_groups(jnp.broadcast_to(q5[:, :, 4:], (ROWS, 4, 4, HEAD))),
        ],
        axis=1,
    )
    got = lax.all_to_all(sent, SPREAD, 0, 0, tiled=True).reshape(4, CHUNKS, KV + 2 * ROWS, HEAD)
    kv = got[:, :, :KV]

    where = jnp.stack([y, zl, 5 * u + group, 5 * u + 4, group]).astype(jnp.int32)
    plans = plan(where, block_count, block_list)
    q = got[:, :, KV:].reshape(4, CHUNKS, 2, ROWS, HEAD)
    q = q.transpose(2, 0, 1, 3, 4).reshape(2 * UNITS, BLOCK, HEAD)

    a01, am0, ap0 = swap(kv), ring_up(kv), ring_down(kv)
    a01, am0, ap0, q, plans = lax.optimization_barrier((a01, am0, ap0, q, plans))
    a11, am1, a20 = swap(ap0), ring_up(a01), ring_down(ap0)
    whole = lambda piece: tuple((piece, name) for name in "kvab")
    state = attend(0, plans, q, (), (kv, a01, am0, ap0), tuple(whole(i) for i in range(4)))
    a11, am1, a20, state = lax.optimization_barrier((a11, am1, a20, state))
    last_k = swap(a20[:, :, :ROWS])
    last_v = ring_up(am1[:, :, ROWS : 2 * ROWS])
    last_e = ring_down(a11[:, :, 2 * ROWS :])
    state = attend(1, plans, q, state, (a11, am1, a20), tuple(whole(i) for i in range(3)))
    out = attend(
        2, plans, q, state, (last_k, last_v, last_e), (((0, "k"),), ((0, "v"),), ((0, "a"), (0, "b")))
    )
    out = lax.all_to_all(out, ("xh", "zh"), 0, 0, tiled=True)

    heads = out[:, :SUPER]
    shares = out[:, SUPER : 2 * SUPER].astype(jnp.float32)
    level = out[:, 2 * SUPER :].reshape(4, 3, STATS, BLOCK)[:, :, :3].astype(jnp.float32)
    level = jnp.sum(level, axis=2).reshape(4, SUPER, 1)
    weight = jnp.exp2(level - jnp.max(level, axis=0, keepdims=True))
    shared = jnp.sum(shares * weight, axis=0) / jnp.sum(weight, axis=0)
    attended = jnp.concatenate(
        [heads.transpose(1, 0, 2).reshape(SUPER, 4 * HEAD), shared.astype(jnp.bfloat16)], axis=1
    )
    return lax.psum_scatter(
        jnp.dot(attended, w_out, preferred_element_type=jnp.float32).astype(jnp.bfloat16),
        ("xl", "c"),
        scatter_dimension=0,
        tiled=True,
    )


def solution(mesh):
    fine = Mesh(mesh.devices.reshape(SIZES), GRID)
    rows = P(NAMES, None)
    return jax.shard_map(
        per_device,
        mesh=fine,
        in_specs=(rows, rows, rows, P(), P(), P(("xl", "c"), None)),
        out_specs=rows,
        check_vma=False,
    )
```

```python
import functools

import jax
import jax.numpy as jnp
from jax import lax
from jax.experimental import pallas as pl
from jax.experimental.pallas import tpu as pltpu
from jax.sharding import Mesh, PartitionSpec as P

HEAD = 128
BLOCK = 128
ROWS = 96
CHUNKS = 4
SUPER = ROWS * CHUNKS
EXT = 32
HALF = 16
KV = 2 * ROWS + 2 * EXT
LOG2E = 1.4426950408889634
SCALE = HEAD ** -0.5 * LOG2E
FLOOR = -1e30
NAMES = ("xh", "zh", "zl", "y", "xl", "c")
GRID = ("xl", "c", "xh", "zh", "zl", "y")
SIZES = (2, 2, 2, 2, 2, 4)
SPREAD = ("xh", "zh", "xl", "c")
STATS = 16
WIDTH = 1280
UNITS = 12
SLOTS = 16
MAIN_GROUP = (2, 2, 2)
EXT_GROUP = (4, 4, 4)
SMEM = pl.BlockSpec(memory_space=pltpu.SMEM)
VMEM = pl.BlockSpec(memory_space=pltpu.VMEM)
HBM = pl.BlockSpec(memory_space=pl.ANY)


def ring_up(x):
    return lax.ppermute(x, "y", [(i, (i + 1) % 4) for i in range(4)])


def ring_down(x):
    return lax.ppermute(x, "y", [(i, (i - 1) % 4) for i in range(4)])


def swap(x):
    return lax.ppermute(x, "zl", [(0, 1), (1, 0)])


def plan_kernel(where_ref, count_ref, table_ref, main_ref, ext0_ref, ext1_ref, n_ref, lists, sem):
    y, zl, head, shared, group = [where_ref[i] for i in range(5)]
    copies = [
        pltpu.make_async_copy(table_ref.at[h], lists.at[i], sem.at[i])
        for i, h in enumerate((head, shared))
    ]
    for copy in copies:
        copy.start()
    for copy in copies:
        copy.wait()

    def unit_step(unit, carry):
        which = lax.div(unit, UNITS)
        local = unit - which * UNITS
        sb = lax.div(local, 3)
        row = (sb * 8 + zl * 4 + y) * 3 + (local - 3 * sb)
        count = count_ref[jnp.where(which == 0, head, shared), row]
        for stage in range(3):
            n_ref[stage, unit] = 0
            for ref in (main_ref, ext0_ref, ext1_ref):
                ref[stage * 24 + unit, 0] = 0

        def slot_step(slot, carry):
            block = lists[which, row, slot]
            sb = lax.div(block, 3)
            r = block - 3 * sb
            column = lax.div(sb, 8)
            zy = sb - 8 * column
            dz = lax.rem(lax.div(zy, 4) + zl, 2)
            dy = lax.rem(lax.rem(zy, 4) + 4 - y, 4)
            stage = jnp.where(
                dz == 0, jnp.where(dy == 2, 1, 0), jnp.where(dy == 0, 0, jnp.where(dy == 2, 2, 1))
            )
            piece = jnp.where(
                dz == 0,
                jnp.where(dy == 0, 0, jnp.where(dy == 3, 2, jnp.where(dy == 1, 3, 2))),
                jnp.where(dy == 0, 1, jnp.where(dy == 3, 1, 0)),
            )
            n = n_ref[stage, unit]
            n_ref[stage, unit] = n + 1
            place = piece * 4 + column
            main_ref[stage * 24 + unit, n] = (place * 3 + r) * BLOCK
            for e, ref in enumerate((ext0_ref, ext1_ref)):
                h = r * 8 + group + 4 * e
                chunk = lax.div(h, 6)
                run = lax.div(h - 6 * chunk, 4)
                ref[stage * 24 + unit, n] = (place * CHUNKS + chunk) * EXT + run * HALF
            return carry

        lax.fori_loop(0, count, slot_step, 0)
        return carry

    lax.fori_loop(0, 2 * UNITS, unit_step, 0)


def plan(where, counts, table):
    lists = jax.ShapeDtypeStruct((72, SLOTS), jnp.int32)
    return pl.pallas_call(
        plan_kernel,
        out_shape=(lists, lists, lists, jax.ShapeDtypeStruct((3, 2 * UNITS), jnp.int32)),
        in_specs=[SMEM, SMEM, HBM],
        out_specs=(SMEM, SMEM, SMEM, SMEM),
        scratch_shapes=[pltpu.SMEM((2, 96, SLOTS), jnp.int32), pltpu.SemaphoreType.DMA((2,))],
        cost_estimate=pl.CostEstimate(flops=8_000_000_000, bytes_accessed=100_000, transcendentals=0),
    )(where, counts, table)


def stage_kernel(stage, shapes, *refs):
    first, last = stage == 0, stage == 2
    where_ref, main_ref, ext0_ref, ext1_ref, n_ref, q_ref = refs[:6]
    refs = refs[6:]
    xl = where_ref[5]
    if not first:
        before = refs[:3]
        refs = refs[3:]
    sources, refs = refs[: len(shapes)], refs[len(shapes) :]
    if last:
        out_ref = refs[0]
        refs = refs[1:]
        k_main, v_main, k_ext, v_ext, sem, top_ref, tot_ref, acc_ref = refs
    else:
        top_ref, tot_ref, acc_ref, k_main, v_main, k_ext, v_ext, sem = refs
    copies = []
    for source, parts in zip(sources, shapes):
        lo = 0
        for piece, name in parts:
            target = {"k": k_main, "v": v_main, "a": k_ext, "b": v_ext}[name]
            rows = ROWS if name in "kv" else EXT
            copy = pltpu.make_async_copy(
                source.at[:, :, pl.ds(lo, rows)], target.at[piece], sem.at[len(copies)]
            )
            copy.start()
            copies.append(copy)
            lo += rows

    def begin(unit, carry):
        if first:
            top_ref[unit] = jnp.full((BLOCK, HEAD), FLOOR, jnp.float32)
            tot_ref[unit] = jnp.zeros((BLOCK, HEAD), jnp.float32)
            acc_ref[unit] = jnp.zeros((BLOCK, HEAD), jnp.float32)
        else:
            for old, new in zip(before, (top_ref, tot_ref, acc_ref)):
                new[unit] = old[unit]
        return carry

    lax.fori_loop(0, 2 * UNITS, begin, 0)
    for copy in copies:
        copy.wait()

    pieces = k_main.shape[0]
    k_flat = k_main.reshape(pieces * 4 * SUPER, HEAD)
    v_flat = v_main.reshape(pieces * 4 * SUPER, HEAD)
    ke_flat = k_ext.reshape(pieces * 4 * CHUNKS * EXT, HEAD)
    ve_flat = v_ext.reshape(pieces * 4 * CHUNKS * EXT, HEAD)
    lane = lax.broadcasted_iota(jnp.int32, (BLOCK, HEAD), 1)
    eye = lax.broadcasted_iota(jnp.int32, (BLOCK, BLOCK), 0) == lane

    def dot_t(a, b):
        return lax.dot_general(a, b, (((1,), (1,)), ((), ())), preferred_element_type=jnp.float32)

    def main_rows(row, slot):
        return [pl.multiple_of(main_ref[row, slot], BLOCK)]

    def ext_rows(row, slot):
        return [pl.multiple_of(ref[row, slot], HALF) for ref in (ext0_ref, ext1_ref)]

    def run(units, group, rows_of, key_flat, value_flat, rows):
        width = len(rows_of(0, 0)) * rows
        ns = [n_ref[stage, unit] for unit in units]
        most = functools.reduce(jnp.maximum, ns)

        def step(t, carry):
            col = lax.broadcasted_iota(jnp.int32, (BLOCK, group * width), 1)
            values, scores = [], []
            for unit, n in zip(units, ns):
                starts = []
                for i in range(group):
                    slot = jnp.maximum(jnp.minimum(group * t + i, n - 1), 0)
                    starts += rows_of(stage * 24 + unit, slot)
                keys = jnp.concatenate([key_flat[pl.ds(r, rows), :] for r in starts], axis=0)
                values.append(
                    jnp.concatenate([value_flat[pl.ds(r, rows), :] for r in starts], axis=0)
                )
                s = dot_t(q_ref[unit], keys)
                scores.append(jnp.where(col < (n - group * t) * width, s, 2 * FLOOR))
            for unit, s, v in zip(units, scores, values):
                top = top_ref[unit][:, :1]
                new_top = jnp.maximum(top, jnp.max(s, axis=1, keepdims=True))
                p = jnp.exp2((s - new_top) * SCALE)
                alpha = jnp.exp2((top - new_top) * SCALE)
                part = functools.reduce(
                    jnp.add, [p[:, i : i + HEAD] for i in range(0, group * width, HEAD)]
                )
                product = jnp.dot(p.astype(jnp.bfloat16), v, preferred_element_type=jnp.float32)
                top_ref[unit] = jnp.broadcast_to(new_top, (BLOCK, HEAD))
                tot_ref[unit] = tot_ref[unit] * alpha + part
                acc_ref[unit] = acc_ref[unit] * alpha + product
            return carry

        lax.fori_loop(0, lax.div(most + (group - 1), group), step, 0)

    def finish(unit):
        total = jnp.sum(tot_ref[unit], axis=1, keepdims=True)
        return top_ref[unit][:, :1], total, (acc_ref[unit] / total).astype(jnp.bfloat16)

    def store(sb, r, top, value):
        for i in range(4):
            granule = 4 * r + i
            chunk = granule // 3
            to = sb if chunk in (0, 3) else jnp.where(xl == 2 - chunk, sb ^ 2, sb)
            place = lax.rem(chunk + 4 - 2 * xl, 4)
            row = pl.multiple_of(top + place * ROWS + (granule % 3) * 32, 32)
            out_ref[to, pl.ds(row, 32), :] = value[32 * i : 32 * i + 32]

    units = list(range(UNITS))
    run(units, MAIN_GROUP[stage], main_rows, k_flat, v_flat, BLOCK)
    if last:
        for unit in units:
            store(unit // 3, unit % 3, 0, finish(unit)[2])
    run([UNITS + unit for unit in units], EXT_GROUP[stage], ext_rows, ke_flat, ve_flat, HALF)
    if last:
        levels = []
        for unit in units:
            top, total, value = finish(UNITS + unit)
            store(unit // 3, unit % 3, SUPER, value)
            level = top * SCALE + jnp.log2(total)
            levels.append(jnp.sum(jnp.where(eye, level, 0.0), axis=0, keepdims=True))
        index = lax.broadcasted_iota(jnp.int32, (STATS, HEAD), 0)
        column = lax.broadcasted_iota(jnp.int32, (1, HEAD), 1)
        for unit in units:
            sb, r = unit // 3, unit % 3
            chunk = (r * BLOCK + column) // ROWS
            level = jnp.where(chunk == 2 - xl, levels[3 * (sb ^ 2) + r], levels[unit])
            high = level.astype(jnp.bfloat16).astype(jnp.float32)
            rest = level - high
            mid = rest.astype(jnp.bfloat16).astype(jnp.float32)
            low = rest - mid
            tile = jnp.where(index == 0, high, jnp.where(index == 1, mid, jnp.where(index == 2, low, 0.0)))
            out_ref[sb, pl.ds(2 * SUPER + r * STATS, STATS), :] = tile.astype(jnp.bfloat16)


def attend(stage, where, plans, q, state, sources, shapes):
    pieces = 1 + max(piece for parts in shapes for piece, _ in parts)
    copies = sum(len(parts) for parts in shapes)
    kept = jax.ShapeDtypeStruct((2 * UNITS, BLOCK, HEAD), jnp.float32)
    scratch = [
        pltpu.VMEM((pieces, 4, CHUNKS, ROWS, HEAD), jnp.bfloat16),
        pltpu.VMEM((pieces, 4, CHUNKS, ROWS, HEAD), jnp.bfloat16),
        pltpu.VMEM((pieces, 4, CHUNKS, EXT, HEAD), jnp.bfloat16),
        pltpu.VMEM((pieces, 4, CHUNKS, EXT, HEAD), jnp.bfloat16),
        pltpu.SemaphoreType.DMA((copies,)),
    ]
    if stage == 2:
        out_shape = jax.ShapeDtypeStruct((4, 2 * SUPER + 3 * STATS, HEAD), jnp.bfloat16)
        out_specs = VMEM
        scratch += [pltpu.VMEM(kept.shape, kept.dtype)] * 3
    else:
        out_shape, out_specs = (kept,) * 3, (VMEM,) * 3
    share = pieces / 8
    return pl.pallas_call(
        functools.partial(stage_kernel, stage, shapes),
        out_shape=out_shape,
        in_specs=[SMEM] * 5 + [VMEM] * (1 + len(state)) + [HBM] * len(sources),
        out_specs=out_specs,
        scratch_shapes=scratch,
        compiler_params=pltpu.CompilerParams(vmem_limit_bytes=32 * 1024 * 1024),
        cost_estimate=pl.CostEstimate(
            flops=int(share * 20e9), bytes_accessed=int(share * 10e6), transcendentals=int(share * 4e6)
        ),
    )(where, *plans, q, *state, *sources)


def around(x, step):
    index = lambda at: (at % 2) * 2 + at % 4 // 2
    return lax.ppermute(x, ("xl", "xh"), [(index(i), index(i + step)) for i in range(4)])


def project_kernel(parts, rows_ref, w_ref, *outs):
    for (chunk, lo, count), out in zip(parts, outs):
        rows = rows_ref[pl.ds(lo, count), :]
        for at in range(0, WIDTH, 256):
            product = jnp.dot(
                rows, w_ref[:, pl.ds(chunk * WIDTH + at, 256)], preferred_element_type=jnp.float32
            )
            out[:, pl.ds(at, 256)] = product.astype(out.dtype)


def project_parts(rows, w, parts):
    return pl.pallas_call(
        functools.partial(project_kernel, parts),
        out_shape=tuple(
            jax.ShapeDtypeStruct((count, WIDTH), jnp.float32 if lo == 0 else jnp.bfloat16)
            for _, lo, count in parts
        ),
        in_specs=[VMEM, VMEM],
        out_specs=(VMEM,) * len(parts),
        compiler_params=pltpu.CompilerParams(vmem_limit_bytes=24 * 1024 * 1024),
        cost_estimate=pl.CostEstimate(
            flops=sum(2 * count * WIDTH * 640 for _, _, count in parts),
            bytes_accessed=4_000_000,
            transcendentals=0,
        ),
    )(rows, w)


def project(rows, w):
    chunks = w.shape[1] // WIDTH
    sides = lambda k: [(k, 2 * ROWS, ROWS), (k, 3 * ROWS, ROWS)]
    own = lambda k: [(k, 0, 2 * ROWS)]
    first = project_parts(rows, w, sides(0))
    rest = project_parts(rows, w, sum([sides(k) for k in range(1, chunks)], []))
    owns = project_parts(rows, w, sum([own(k) for k in range(chunks)], []))
    sent = first + rest
    return sent[0::2], sent[1::2], owns


def to_groups(main):
    rows = main.shape[0]
    return main.transpose(2, 1, 0, 3).reshape(16, rows, HEAD)


def shared_keys(rows, core):
    runs = jnp.pad(rows, ((0, 32), (0, 0), (0, 0))).reshape(2, 4, HALF, 4, HEAD)
    runs = jnp.where(core == 0, runs, jnp.roll(runs, 2, axis=1))
    return runs.transpose(1, 3, 0, 2, 4).reshape(16, EXT, HEAD)


def per_device(queries, key_rows, value_rows, block_list, block_count, w_out):
    xh, zh, zl, y, xl, c = [lax.axis_index(name) for name in NAMES]
    u = 2 * xl + c
    group = 2 * xh + zh
    k5 = key_rows.reshape(ROWS, 4, 5, HEAD)
    v5 = value_rows.reshape(ROWS, 4, 5, HEAD)
    q5 = queries.reshape(ROWS, 4, 5, HEAD)
    sent = jnp.concatenate(
        [
            to_groups(k5[:, :, :4]),
            to_groups(v5[:, :, :4]),
            shared_keys(k5[:, :, 4], c),
            shared_keys(v5[:, :, 4], c),
            to_groups(q5[:, :, :4]),
            to_groups(jnp.broadcast_to(q5[:, :, 4:], (ROWS, 4, 4, HEAD))),
        ],
        axis=1,
    )
    got = lax.all_to_all(sent, SPREAD, 0, 0, tiled=True).reshape(4, CHUNKS, KV + 2 * ROWS, HEAD)
    kv = got[:, :, :KV]

    where = jnp.stack([y, zl, 5 * u + group, 5 * u + 4, group, xl]).astype(jnp.int32)
    plans = plan(where, block_count, block_list)
    q = got[:, :, KV:].reshape(4, CHUNKS, 2, ROWS, HEAD)
    q = q.transpose(2, 0, 1, 3, 4).reshape(2 * UNITS, BLOCK, HEAD)

    a01, am0, ap0 = swap(kv), ring_up(kv), ring_down(kv)
    a01, am0, ap0, q, plans = lax.optimization_barrier((a01, am0, ap0, q, plans))
    a11, am1, a20 = swap(ap0), ring_up(a01), ring_down(ap0)
    whole = lambda piece: tuple((piece, name) for name in "kvab")
    state = attend(0, where, plans, q, (), (kv, a01, am0, ap0), tuple(whole(i) for i in range(4)))
    a11, am1, a20, state = lax.optimization_barrier((a11, am1, a20, state))
    last_k = swap(a20[:, :, :ROWS])
    last_v = ring_up(am1[:, :, ROWS : 2 * ROWS])
    last_e = ring_down(a11[:, :, 2 * ROWS :])
    state = attend(1, where, plans, q, state, (a11, am1, a20), tuple(whole(i) for i in range(3)))
    out = attend(
        2, where, plans, q, state, (last_k, last_v, last_e), (((0, "k"),), ((0, "v"),), ((0, "a"), (0, "b")))
    )
    out = lax.all_to_all(out, ("xh", "zh"), 0, 0, tiled=True)

    heads = out[:, :SUPER]
    shares = out[:, SUPER : 2 * SUPER].astype(jnp.float32)
    level = out[:, 2 * SUPER :].reshape(4, 3, STATS, BLOCK)[:, :, :3].astype(jnp.float32)
    level = jnp.sum(level, axis=2).reshape(4, SUPER)
    level = jnp.where(xl == 0, level, jnp.roll(level, 2 * ROWS, axis=1))[:, :, None]
    weight = jnp.exp2(level - jnp.max(level, axis=0, keepdims=True))
    shared = jnp.sum(shares * weight, axis=0) / jnp.sum(weight, axis=0)
    attended = jnp.concatenate(
        [heads.transpose(1, 0, 2).reshape(SUPER, 4 * HEAD), shared.astype(jnp.bfloat16)], axis=1
    )
    lows, highs, owns = project(attended, w_out)
    total = []
    for low, high, own in zip(lows, highs, owns):
        first = own[:ROWS] + around(low, -1).astype(jnp.float32)
        second = own[ROWS:] + around(high, 1).astype(jnp.float32)
        keep = jnp.where(c == 0, first, second)
        give = jnp.where(c == 0, second, first).astype(jnp.bfloat16)
        total.append((keep + lax.ppermute(give, "c", [(0, 1), (1, 0)])).astype(jnp.bfloat16))
    return jnp.concatenate(total, axis=1)


def solution(mesh):
    fine = Mesh(mesh.devices.reshape(SIZES), GRID)
    rows = P(NAMES, None)
    return jax.shard_map(
        per_device,
        mesh=fine,
        in_specs=(rows, rows, rows, P(), P(), P(("xl", "c"), None)),
        out_specs=rows,
        check_vma=False,
    )
```

```python
import functools

import jax
import jax.numpy as jnp
from jax import lax
from jax.experimental import pallas as pl
from jax.experimental.pallas import tpu as pltpu
from jax.sharding import Mesh, PartitionSpec as P

HEAD = 128
BLOCK = 128
ROWS = 96
CHUNKS = 4
SUPER = ROWS * CHUNKS
RUN = 16
MAIN = ROWS // 2
EXT = RUN
PART = MAIN + EXT
KV = 2 * PART
LOG2E = 1.4426950408889634
SCALE = HEAD ** -0.5 * LOG2E
FLOOR = -1e30
NAMES = ("xh", "zh", "zl", "y", "xl", "c")
GRID = ("xl", "c", "xh", "zh", "zl", "y")
SIZES = (2, 2, 2, 2, 2, 4)
SPREAD = ("xh", "zh", "zl", "xl", "c")
COLS = 8
UNITS = 3 * COLS
SLOTS = 16
MAIN_GROUP = 4
EXT_GROUP = 8
BATCH = 12
STATS = 16
WIDTH = 1280
SMEM = pl.BlockSpec(memory_space=pltpu.SMEM)
VMEM = pl.BlockSpec(memory_space=pltpu.VMEM)
HBM = pl.BlockSpec(memory_space=pl.ANY)


def ring_up(x):
    return lax.ppermute(x, "y", [(i, (i + 1) % 4) for i in range(4)])


def ring_down(x):
    return lax.ppermute(x, "y", [(i, (i - 1) % 4) for i in range(4)])


def plan_kernel(where_ref, count_ref, table_ref, start_ref, n_ref, lists, sem):
    y, head, shared, share = [where_ref[i] for i in range(4)]
    copies = [
        pltpu.make_async_copy(table_ref.at[h], lists.at[i], sem.at[i])
        for i, h in enumerate((head, shared))
    ]
    for copy in copies:
        copy.start()
    for copy in copies:
        copy.wait()

    for which, h in enumerate((head, shared)):

        def unit_step(local, carry):
            unit = which * UNITS + local
            column = (local * 171) >> 9
            row = (column * 4 + y) * 3 + (local - 3 * column)
            start_ref[unit, 0] = 0
            start_ref[2 * UNITS + unit, 0] = 0

            def slot_step(slot, found):
                block = lists[which, row, slot]
                sb = (block * 171) >> 9
                r = block - 3 * sb
                dy = ((sb & 3) + 4 - y) & 3
                late = dy == 2
                place = jnp.where(late, 0, (4 - dy) & 3) - jnp.where(dy == 1, 1, 0)
                place = place * COLS + (sb >> 2)
                if which == 0:
                    start = place * (CHUNKS * MAIN) + r * (BLOCK // 2)
                else:
                    chunk = ((r * 8 + share) * 43) >> 8
                    start = (place * CHUNKS + chunk) * EXT
                early_n, late_n = found
                start_ref[jnp.where(late, 2 * UNITS, 0) + unit, jnp.where(late, late_n, early_n)] = start
                step = late.astype(jnp.int32)
                return early_n + 1 - step, late_n + step

            zero = jnp.int32(0)
            early_n, late_n = lax.fori_loop(0, count_ref[h, row], slot_step, (zero, zero))
            n_ref[0, unit] = early_n
            n_ref[1, unit] = late_n
            return carry

        lax.fori_loop(0, UNITS, unit_step, 0)


def plan(where, counts, table):
    return pl.pallas_call(
        plan_kernel,
        out_shape=(
            jax.ShapeDtypeStruct((4 * UNITS, SLOTS), jnp.int32),
            jax.ShapeDtypeStruct((2, 2 * UNITS), jnp.int32),
        ),
        in_specs=[SMEM, SMEM, HBM],
        out_specs=(SMEM, SMEM),
        scratch_shapes=[pltpu.SMEM((2, 96, SLOTS), jnp.int32), pltpu.SemaphoreType.DMA((2,))],
        cost_estimate=pl.CostEstimate(flops=8_000_000_000, bytes_accessed=100_000, transcendentals=0),
    )(where, counts, table)


def stage_kernel(last, pieces, *refs):
    where_ref, start_ref, n_ref, q_ref = refs[:4]
    refs = refs[4:]
    xl = where_ref[4]
    if last:
        before, (last_k, last_v, out_ref), refs = refs[:3], refs[3:6], refs[6:]
        k_main, v_main, k_ext, v_ext, sem, top_ref, tot_ref, acc_ref = refs
        loads = [(last_k, 0, 0, k_main, k_ext), (last_v, 0, 0, v_main, v_ext)]
    else:
        sources, refs = refs[:pieces], refs[pieces:]
        top_ref, tot_ref, acc_ref, k_main, v_main, k_ext, v_ext, sem = refs
        loads = []
        for i, source in enumerate(sources):
            loads += [(source, 0, i, k_main, k_ext), (source, PART, i, v_main, v_ext)]
    stage = 1 if last else 0
    first = not last
    copies = []
    for source, lo, piece, main, ext in loads:
        for target, at, rows in ((main, lo, MAIN), (ext, lo + MAIN, EXT)):
            copy = pltpu.make_async_copy(
                source.at[:, :, pl.ds(at, rows)], target.at[piece], sem.at[len(copies)]
            )
            copy.start()
            copies.append(copy)

    def begin(unit, carry):
        if first:
            top_ref[unit] = jnp.full((BLOCK, HEAD), FLOOR, jnp.float32)
            tot_ref[unit] = jnp.zeros((BLOCK, HEAD), jnp.float32)
            acc_ref[unit] = jnp.zeros((BLOCK, HEAD), jnp.float32)
        else:
            for old, new in zip(before, (top_ref, tot_ref, acc_ref)):
                new[unit] = old[unit]
        return carry

    lax.fori_loop(0, 2 * UNITS, begin, 0)
    for copy in copies:
        copy.wait()

    k_flat = k_main.reshape(pieces * COLS * CHUNKS * MAIN, HEAD)
    v_flat = v_main.reshape(pieces * COLS * CHUNKS * MAIN, HEAD)
    ke_flat = k_ext.reshape(pieces * COLS * CHUNKS * EXT, HEAD)
    ve_flat = v_ext.reshape(pieces * COLS * CHUNKS * EXT, HEAD)
    lane = lax.broadcasted_iota(jnp.int32, (BLOCK, HEAD), 1)
    eye = lax.broadcasted_iota(jnp.int32, (BLOCK, BLOCK), 0) == lane

    def dot_t(a, b):
        return lax.dot_general(a, b, (((1,), (1,)), ((), ())), preferred_element_type=jnp.float32)

    def run(units, group, key_flat, value_flat, width):
        ns = [n_ref[stage, unit] for unit in units]
        most = functools.reduce(jnp.maximum, ns)

        def step(t, carry):
            col = lax.broadcasted_iota(jnp.int32, (BLOCK, group * width), 1)
            values, scores = [], []
            for unit, n in zip(units, ns):
                starts = []
                for i in range(group):
                    slot = jnp.maximum(jnp.minimum(group * t + i, n - 1), 0)
                    start = start_ref[stage * 2 * UNITS + unit, slot]
                    starts.append(pl.multiple_of(start, width))
                keys = jnp.concatenate([key_flat[pl.ds(r, width), :] for r in starts], axis=0)
                values.append(
                    jnp.concatenate([value_flat[pl.ds(r, width), :] for r in starts], axis=0)
                )
                s = dot_t(q_ref[unit], keys)
                scores.append(jnp.where(col < (n - group * t) * width, s, 2 * FLOOR))
            for unit, s, v in zip(units, scores, values):
                top = top_ref[unit][:, :1]
                new_top = jnp.maximum(top, jnp.max(s, axis=1, keepdims=True))
                p = jnp.exp2((s - new_top) * SCALE)
                alpha = jnp.exp2((top - new_top) * SCALE)
                part = functools.reduce(
                    jnp.add, [p[:, i : i + HEAD] for i in range(0, group * width, HEAD)]
                )
                product = jnp.dot(p.astype(jnp.bfloat16), v, preferred_element_type=jnp.float32)
                top_ref[unit] = jnp.broadcast_to(new_top, (BLOCK, HEAD))
                tot_ref[unit] = tot_ref[unit] * alpha + part
                acc_ref[unit] = acc_ref[unit] * alpha + product
            return carry

        lax.fori_loop(0, lax.div(most + (group - 1), group), step, 0)

    def finish(unit):
        total = jnp.sum(tot_ref[unit], axis=1, keepdims=True)
        return top_ref[unit][:, :1], total, (acc_ref[unit] / total).astype(jnp.bfloat16)

    def store(sb, r, top, value):
        for i in range(4):
            granule = 4 * r + i
            chunk = granule // 3
            to = sb if chunk in (0, 3) else jnp.where(xl == 2 - chunk, sb ^ 4, sb)
            place = lax.rem(chunk + 4 - 2 * xl, 4)
            row = pl.multiple_of(top + place * ROWS + (granule % 3) * 32, 32)
            out_ref[to, pl.ds(row, 32), :] = value[32 * i : 32 * i + 32]

    levels = [[], []]
    for which in range(2):
        for lo in range(0, UNITS, BATCH):
            units = range(which * UNITS + lo, which * UNITS + lo + BATCH)
            if which == 0:
                run(units, MAIN_GROUP, k_flat, v_flat, BLOCK // 2)
            else:
                run(units, EXT_GROUP, ke_flat, ve_flat, RUN)
            if not last:
                continue
            for unit in units:
                top, total, value = finish(unit)
                local = unit - which * UNITS
                store(local // 3, local % 3, which * SUPER, value)
                level = top * SCALE + jnp.log2(total)
                levels[which].append(jnp.sum(jnp.where(eye, level, 0.0), axis=0, keepdims=True))
    if not last:
        return
    index = lax.broadcasted_iota(jnp.int32, (STATS, HEAD), 0)
    column = lax.broadcasted_iota(jnp.int32, (1, HEAD), 1)
    for unit in range(UNITS):
        sb, r = unit // 3, unit % 3
        chunk = (r * BLOCK + column) // ROWS
        tile = jnp.zeros((STATS, HEAD), jnp.float32)
        for which in range(2):
            level = jnp.where(chunk == 2 - xl, levels[which][3 * (sb ^ 4) + r], levels[which][unit])
            for i in range(3):
                term = level.astype(jnp.bfloat16).astype(jnp.float32)
                tile = jnp.where(index == 3 * which + i, term, tile)
                level = level - term
        out_ref[sb, pl.ds(2 * SUPER + r * STATS, STATS), :] = tile.astype(jnp.bfloat16)


def attend(last, where, plans, q, state, sources):
    pieces = 1 if last else len(sources)
    kept = jax.ShapeDtypeStruct((2 * UNITS, BLOCK, HEAD), jnp.float32)
    scratch = [
        pltpu.VMEM((pieces, COLS, CHUNKS, MAIN, HEAD), jnp.bfloat16),
        pltpu.VMEM((pieces, COLS, CHUNKS, MAIN, HEAD), jnp.bfloat16),
        pltpu.VMEM((pieces, COLS, CHUNKS, EXT, HEAD), jnp.bfloat16),
        pltpu.VMEM((pieces, COLS, CHUNKS, EXT, HEAD), jnp.bfloat16),
        pltpu.SemaphoreType.DMA((4 * pieces,)),
    ]
    if last:
        out_shape = jax.ShapeDtypeStruct((COLS, 2 * SUPER + 3 * STATS, HEAD), jnp.bfloat16)
        out_specs = VMEM
        scratch += [pltpu.VMEM(kept.shape, kept.dtype)] * 3
    else:
        out_shape, out_specs = (kept,) * 3, (VMEM,) * 3
    return pl.pallas_call(
        functools.partial(stage_kernel, last, pieces),
        out_shape=out_shape,
        in_specs=[SMEM] * 3 + [VMEM] * (1 + len(state)) + [HBM] * len(sources),
        out_specs=out_specs,
        scratch_shapes=scratch,
        compiler_params=pltpu.CompilerParams(vmem_limit_bytes=32 * 1024 * 1024),
        cost_estimate=pl.CostEstimate(
            flops=pieces * 5_000_000_000, bytes_accessed=pieces * 2_000_000, transcendentals=1_000_000
        ),
    )(where, *plans, q, *state, *sources)


def around(x, step):
    index = lambda at: (at % 2) * 2 + at % 4 // 2
    return lax.ppermute(x, ("xl", "xh"), [(index(i), index(i + step)) for i in range(4)])


def project_kernel(parts, rows_ref, w_ref, *outs):
    for (chunk, lo, count), out in zip(parts, outs):
        rows = rows_ref[pl.ds(lo, count), :]
        for at in range(0, WIDTH, 256):
            product = jnp.dot(
                rows, w_ref[:, pl.ds(chunk * WIDTH + at, 256)], preferred_element_type=jnp.float32
            )
            out[:, pl.ds(at, 256)] = product.astype(out.dtype)


def project_parts(rows, w, parts):
    return pl.pallas_call(
        functools.partial(project_kernel, parts),
        out_shape=tuple(
            jax.ShapeDtypeStruct((count, WIDTH), jnp.float32 if lo == 0 else jnp.bfloat16)
            for _, lo, count in parts
        ),
        in_specs=[VMEM, VMEM],
        out_specs=(VMEM,) * len(parts),
        compiler_params=pltpu.CompilerParams(vmem_limit_bytes=24 * 1024 * 1024),
        cost_estimate=pl.CostEstimate(
            flops=sum(2 * count * WIDTH * 640 for _, _, count in parts),
            bytes_accessed=4_000_000,
            transcendentals=0,
        ),
    )(rows, w)


def project(rows, w):
    chunks = w.shape[1] // WIDTH
    sides = lambda k: [(k, 2 * ROWS, ROWS), (k, 3 * ROWS, ROWS)]
    own = lambda k: [(k, 0, 2 * ROWS)]
    first = project_parts(rows, w, sides(0))
    rest = project_parts(rows, w, sum([sides(k) for k in range(1, chunks)], []))
    owns = project_parts(rows, w, sum([own(k) for k in range(chunks)], []))
    sent = first + rest
    return sent[0::2], sent[1::2], owns


def main_keys(rows):
    runs = rows.reshape(3, 2, RUN, 4, 4, HEAD).transpose(4, 1, 3, 0, 2, 5)
    return runs.reshape(32, MAIN, HEAD)


def shared_keys(rows, xl, c):
    runs = jnp.pad(rows, ((0, 32), (0, 0), (0, 0))).reshape(8, RUN, 4, HEAD)
    runs = jnp.where(xl == 0, runs, jnp.roll(runs, -4, axis=0))
    runs = jnp.where(c == 0, runs, jnp.roll(runs, -2, axis=0))
    return runs.transpose(0, 2, 1, 3).reshape(32, EXT, HEAD)


def merge(shares, levels):
    weights = jnp.exp2(levels - jnp.max(levels, axis=1, keepdims=True))
    weights = weights / jnp.sum(weights, axis=1, keepdims=True)
    return jnp.sum(shares.astype(jnp.float32) * weights[..., None], axis=1).astype(jnp.bfloat16)


def per_device(queries, key_rows, value_rows, block_list, block_count, w_out):
    xh, zh, zl, y, xl, c = [lax.axis_index(name) for name in NAMES]
    u = 2 * xl + c
    j = 2 * xh + zh
    k5 = key_rows.reshape(ROWS, 4, 5, HEAD)
    v5 = value_rows.reshape(ROWS, 4, 5, HEAD)
    q5 = queries.reshape(ROWS, 4, 5, HEAD)
    sent = jnp.concatenate(
        [
            main_keys(k5[:, :, :4]),
            shared_keys(k5[:, :, 4], xl, c),
            main_keys(v5[:, :, :4]),
            shared_keys(v5[:, :, 4], xl, c),
        ],
        axis=1,
    )
    kv = lax.all_to_all(sent, SPREAD, 0, 0, tiled=True).reshape(COLS, CHUNKS, KV, HEAD)

    q = jnp.stack([q5[:, :, :4], jnp.broadcast_to(q5[:, :, 4:], (ROWS, 4, 4, HEAD))])
    q = jnp.broadcast_to(q.transpose(3, 2, 0, 1, 4)[:, None], (4, 2, 4, 2, ROWS, HEAD))
    q = lax.all_to_all(q.reshape(32, 2, ROWS, HEAD), SPREAD, 0, 0, tiled=True)
    q = q.reshape(COLS, CHUNKS, 2, ROWS, HEAD).transpose(2, 0, 1, 3, 4).reshape(2 * UNITS, BLOCK, HEAD)

    where = jnp.stack([y, 5 * u + j, 5 * u + 4, 2 * j + zl, xl]).astype(jnp.int32)
    plans = plan(where, block_count, block_list)

    below, above = ring_up(kv), ring_down(kv)
    below, above, q, plans = lax.optimization_barrier((below, above, q, plans))
    last_k = ring_down(above[:, :, :PART])
    last_v = ring_up(below[:, :, PART:])
    state = attend(False, where, plans, q, (), (kv, below, above))
    out = attend(True, where, plans, q, state, (last_k, last_v))
    out = lax.all_to_all(out, ("xh", "zh", "zl"), 0, 0, tiled=True)

    levels = out[:, 2 * SUPER :].reshape(COLS, 3, STATS, BLOCK)[:, :, :6].astype(jnp.float32)
    levels = jnp.sum(levels.reshape(COLS, 3, 2, 3, BLOCK), axis=3).transpose(2, 0, 1, 3)
    levels = levels.reshape(2, COLS, SUPER)
    levels = jnp.where(xl == 0, levels, jnp.roll(levels, 2 * ROWS, axis=2))
    heads = merge(out[:, :SUPER].reshape(4, 2, SUPER, HEAD), levels[0].reshape(4, 2, SUPER))
    shared = merge(out[None, :, SUPER : 2 * SUPER], levels[1][None])
    attended = jnp.concatenate([heads, shared], axis=0).transpose(1, 0, 2).reshape(SUPER, 5 * HEAD)

    lows, highs, owns = project(attended, w_out)
    total = []
    for low, high, own in zip(lows, highs, owns):
        first = own[:ROWS] + around(low, -1).astype(jnp.float32)
        second = own[ROWS:] + around(high, 1).astype(jnp.float32)
        keep = jnp.where(c == 0, first, second)
        give = jnp.where(c == 0, second, first).astype(jnp.bfloat16)
        total.append((keep + lax.ppermute(give, "c", [(0, 1), (1, 0)])).astype(jnp.bfloat16))
    return jnp.concatenate(total, axis=1)


def solution(mesh):
    fine = Mesh(mesh.devices.reshape(SIZES), GRID)
    rows = P(NAMES, None)
    return jax.shard_map(
        per_device,
        mesh=fine,
        in_specs=(rows, rows, rows, P(), P(), P(("xl", "c"), None)),
        out_specs=rows,
        check_vma=False,
    )
```

```python
import functools

import jax
import jax.numpy as jnp
from jax import lax
from jax.experimental import pallas as pl
from jax.experimental.pallas import tpu as pltpu
from jax.sharding import Mesh, PartitionSpec as P

HEAD = 128
BLOCK = 128
ROWS = 96
CHUNKS = 4
SUPER = ROWS * CHUNKS
RUN = 16
MAIN = ROWS // 2
EXT = RUN
PART = MAIN + EXT
KV = 2 * PART
LOG2E = 1.4426950408889634
SCALE = HEAD ** -0.5 * LOG2E
FLOOR = -1e30
NAMES = ("xh", "zh", "zl", "y", "xl", "c")
GRID = ("xl", "c", "xh", "zh", "zl", "y")
SIZES = (2, 2, 2, 2, 2, 4)
SPREAD = ("xh", "zh", "zl", "xl", "c")
COLS = 8
UNITS = 3 * COLS
SLOTS = 16
MAIN_GROUP = 4
EXT_GROUP = 8
BATCH = 12
STATS = 16
WIDTH = 1280
SMEM = pl.BlockSpec(memory_space=pltpu.SMEM)
VMEM = pl.BlockSpec(memory_space=pltpu.VMEM)
HBM = pl.BlockSpec(memory_space=pl.ANY)


def ring_up(x):
    return lax.ppermute(x, "y", [(i, (i + 1) % 4) for i in range(4)])


def ring_down(x):
    return lax.ppermute(x, "y", [(i, (i - 1) % 4) for i in range(4)])


def plan_kernel(where_ref, count_ref, table_ref, start_ref, n_ref, lists, sem):
    y, head, shared, share = [where_ref[i] for i in range(4)]
    copies = [
        pltpu.make_async_copy(table_ref.at[h], lists.at[i], sem.at[i])
        for i, h in enumerate((head, shared))
    ]
    for copy in copies:
        copy.start()
    for copy in copies:
        copy.wait()

    for which, h in enumerate((head, shared)):

        def unit_step(local, carry):
            unit = which * UNITS + local
            column = (local * 171) >> 9
            row = (column * 4 + y) * 3 + (local - 3 * column)
            start_ref[unit, 0] = 0
            start_ref[2 * UNITS + unit, 0] = 0

            def slot_step(slot, found):
                block = lists[which, row, slot]
                sb = (block * 171) >> 9
                r = block - 3 * sb
                dy = ((sb & 3) + 4 - y) & 3
                late = dy == 2
                place = jnp.where(late, 0, (4 - dy) & 3) - jnp.where(dy == 1, 1, 0)
                place = place * COLS + (sb >> 2)
                if which == 0:
                    start = place * (CHUNKS * MAIN) + r * (BLOCK // 2)
                else:
                    chunk = ((r * 8 + share) * 43) >> 8
                    start = (place * CHUNKS + chunk) * EXT
                early_n, late_n = found
                start_ref[jnp.where(late, 2 * UNITS, 0) + unit, jnp.where(late, late_n, early_n)] = start
                step = late.astype(jnp.int32)
                return early_n + 1 - step, late_n + step

            zero = jnp.int32(0)
            early_n, late_n = lax.fori_loop(0, count_ref[h, row], slot_step, (zero, zero))
            n_ref[0, unit] = early_n
            n_ref[1, unit] = late_n
            return carry

        lax.fori_loop(0, UNITS, unit_step, 0)


def plan(where, counts, table):
    return pl.pallas_call(
        plan_kernel,
        out_shape=(
            jax.ShapeDtypeStruct((4 * UNITS, SLOTS), jnp.int32),
            jax.ShapeDtypeStruct((2, 2 * UNITS), jnp.int32),
        ),
        in_specs=[SMEM, SMEM, HBM],
        out_specs=(SMEM, SMEM),
        scratch_shapes=[pltpu.SMEM((2, 96, SLOTS), jnp.int32), pltpu.SemaphoreType.DMA((2,))],
        cost_estimate=pl.CostEstimate(flops=8_000_000_000, bytes_accessed=100_000, transcendentals=0),
    )(where, counts, table)


def stage_kernel(last, pieces, *refs):
    where_ref, start_ref, n_ref, q_ref = refs[:4]
    refs = refs[4:]
    xl = where_ref[4]
    if last:
        before, (last_k, last_v, out_ref), refs = refs[:3], refs[3:6], refs[6:]
        k_main, v_main, k_ext, v_ext, sem, top_ref, tot_ref, acc_ref = refs
        loads = [(last_k, 0, 0, k_main, k_ext), (last_v, 0, 0, v_main, v_ext)]
    else:
        sources, refs = refs[:pieces], refs[pieces:]
        top_ref, tot_ref, acc_ref, k_main, v_main, k_ext, v_ext, sem = refs
        loads = []
        for i, source in enumerate(sources):
            loads += [(source, 0, i, k_main, k_ext), (source, PART, i, v_main, v_ext)]
    stage = 1 if last else 0
    first = not last
    state = (top_ref, tot_ref, acc_ref)
    copies = []
    for source, lo, piece, main, ext in loads:
        for target, at, rows in ((main, lo, MAIN), (ext, lo + MAIN, EXT)):
            copy = pltpu.make_async_copy(
                source.at[:, :, pl.ds(at, rows)], target.at[piece], sem.at[len(copies)]
            )
            copy.start()
            copies.append(copy)

    for copy in copies:
        copy.wait()

    k_flat = k_main.reshape(pieces * COLS * CHUNKS * MAIN, HEAD)
    v_flat = v_main.reshape(pieces * COLS * CHUNKS * MAIN, HEAD)
    ke_flat = k_ext.reshape(pieces * COLS * CHUNKS * EXT, HEAD)
    ve_flat = v_ext.reshape(pieces * COLS * CHUNKS * EXT, HEAD)
    lane = lax.broadcasted_iota(jnp.int32, (BLOCK, HEAD), 1)
    eye = lax.broadcasted_iota(jnp.int32, (BLOCK, BLOCK), 0) == lane

    def dot_t(a, b):
        return lax.dot_general(a, b, (((1,), (1,)), ((), ())), preferred_element_type=jnp.float32)

    def run(units, group, key_flat, value_flat, width):
        ns = [n_ref[stage, unit] for unit in units]
        most = functools.reduce(jnp.maximum, ns)

        def step(t, carry, start=False):
            col = lax.broadcasted_iota(jnp.int32, (1, group * width), 1)
            values, scores = [], []
            for unit, n in zip(units, ns):
                starts = []
                for i in range(group):
                    slot = jnp.maximum(jnp.minimum(group * t + i, n - 1), 0)
                    at = start_ref[stage * 2 * UNITS + unit, slot]
                    starts.append(pl.multiple_of(at, width))
                keys = jnp.concatenate([key_flat[pl.ds(r, width), :] for r in starts], axis=0)
                values.append(
                    jnp.concatenate([value_flat[pl.ds(r, width), :] for r in starts], axis=0)
                )
                bias = jnp.where(col < (n - group * t) * width, 0.0, 2 * FLOOR)
                scores.append(dot_t(q_ref[unit], keys) + bias)
            for unit, s, v in zip(units, scores, values):
                parts = [s[:, i : i + HEAD] for i in range(0, group * width, HEAD)]
                peak = jnp.max(functools.reduce(jnp.maximum, parts), axis=1, keepdims=True)
                if start and first:
                    new_top = jnp.maximum(jnp.broadcast_to(peak, (BLOCK, HEAD)), FLOOR)
                else:
                    top, tot, acc = [ref[unit] for ref in (before if start else state)]
                    new_top = jnp.maximum(top, peak)
                weights = [jnp.exp2((part - new_top) * SCALE) for part in parts]
                low = jnp.concatenate([w.astype(jnp.bfloat16) for w in weights], axis=1)
                product = jnp.dot(low, v, preferred_element_type=jnp.float32)
                total = functools.reduce(jnp.add, weights)
                if not (start and first):
                    alpha = jnp.exp2((top - new_top) * SCALE)
                    total = tot * alpha + total
                    product = acc * alpha + product
                top_ref[unit] = new_top
                tot_ref[unit] = total
                acc_ref[unit] = product
            return carry

        step(0, 0, True)
        lax.fori_loop(1, lax.div(most + (group - 1), group), step, 0)

    def finish(unit):
        total = jnp.sum(tot_ref[unit], axis=1, keepdims=True)
        return top_ref[unit], total, (acc_ref[unit] / total).astype(jnp.bfloat16)

    def store(sb, r, top, value):
        for i in range(4):
            granule = 4 * r + i
            chunk = granule // 3
            to = sb if chunk in (0, 3) else jnp.where(xl == 2 - chunk, sb ^ 4, sb)
            place = lax.rem(chunk + 4 - 2 * xl, 4)
            row = pl.multiple_of(top + place * ROWS + (granule % 3) * 32, 32)
            out_ref[to, pl.ds(row, 32), :] = value[32 * i : 32 * i + 32]

    levels = [[], []]
    for which in range(2):
        for lo in range(0, UNITS, BATCH):
            units = range(which * UNITS + lo, which * UNITS + lo + BATCH)
            if which == 0:
                run(units, MAIN_GROUP, k_flat, v_flat, BLOCK // 2)
            else:
                run(units, EXT_GROUP, ke_flat, ve_flat, RUN)
            if not last:
                continue
            for unit in units:
                top, total, value = finish(unit)
                local = unit - which * UNITS
                store(local // 3, local % 3, which * SUPER, value)
                level = top * SCALE + jnp.log2(total)
                levels[which].append(jnp.sum(jnp.where(eye, level, 0.0), axis=0, keepdims=True))
    if not last:
        return
    index = lax.broadcasted_iota(jnp.int32, (STATS, HEAD), 0)
    column = lax.broadcasted_iota(jnp.int32, (1, HEAD), 1)
    for unit in range(UNITS):
        sb, r = unit // 3, unit % 3
        chunk = (r * BLOCK + column) // ROWS
        tile = jnp.zeros((STATS, HEAD), jnp.float32)
        for which in range(2):
            level = jnp.where(chunk == 2 - xl, levels[which][3 * (sb ^ 4) + r], levels[which][unit])
            for i in range(3):
                term = level.astype(jnp.bfloat16).astype(jnp.float32)
                tile = jnp.where(index == 3 * which + i, term, tile)
                level = level - term
        out_ref[sb, pl.ds(2 * SUPER + r * STATS, STATS), :] = tile.astype(jnp.bfloat16)


def attend(last, where, plans, q, state, sources):
    pieces = 1 if last else len(sources)
    kept = jax.ShapeDtypeStruct((2 * UNITS, BLOCK, HEAD), jnp.float32)
    scratch = [
        pltpu.VMEM((pieces, COLS, CHUNKS, MAIN, HEAD), jnp.bfloat16),
        pltpu.VMEM((pieces, COLS, CHUNKS, MAIN, HEAD), jnp.bfloat16),
        pltpu.VMEM((pieces, COLS, CHUNKS, EXT, HEAD), jnp.bfloat16),
        pltpu.VMEM((pieces, COLS, CHUNKS, EXT, HEAD), jnp.bfloat16),
        pltpu.SemaphoreType.DMA((4 * pieces,)),
    ]
    if last:
        out_shape = jax.ShapeDtypeStruct((COLS, 2 * SUPER + 3 * STATS, HEAD), jnp.bfloat16)
        out_specs = VMEM
        scratch += [pltpu.VMEM(kept.shape, kept.dtype)] * 3
    else:
        out_shape, out_specs = (kept,) * 3, (VMEM,) * 3
    return pl.pallas_call(
        functools.partial(stage_kernel, last, pieces),
        out_shape=out_shape,
        in_specs=[SMEM] * 3 + [VMEM] * (1 + len(state)) + [HBM] * len(sources),
        out_specs=out_specs,
        scratch_shapes=scratch,
        compiler_params=pltpu.CompilerParams(vmem_limit_bytes=32 * 1024 * 1024),
        cost_estimate=pl.CostEstimate(
            flops=pieces * 5_000_000_000, bytes_accessed=pieces * 2_000_000, transcendentals=1_000_000
        ),
    )(where, *plans, q, *state, *sources)


def around(x, step):
    index = lambda at: (at % 2) * 2 + at % 4 // 2
    return lax.ppermute(x, ("xl", "xh"), [(index(i), index(i + step)) for i in range(4)])


def project_kernel(parts, rows_ref, w_ref, *refs):
    outs, (w_buf, sem) = refs[:-2], refs[-2:]
    chunks = sorted({chunk for chunk, _, _ in parts})
    copies = {}
    for i, chunk in enumerate(chunks):
        copies[chunk] = pltpu.make_async_copy(
            w_ref.at[:, pl.ds(chunk * WIDTH, WIDTH)], w_buf.at[i], sem.at[i]
        )
        copies[chunk].start()
    for i, chunk in enumerate(chunks):
        copies[chunk].wait()
        for (which, lo, count), out in zip(parts, outs):
            if which != chunk:
                continue
            rows = rows_ref[pl.ds(lo, count), :]
            for at in range(0, WIDTH, 256):
                product = jnp.dot(
                    rows, w_buf[i, :, pl.ds(at, 256)], preferred_element_type=jnp.float32
                )
                out[:, pl.ds(at, 256)] = product.astype(out.dtype)


def project_parts(rows, w, parts):
    chunks = len({chunk for chunk, _, _ in parts})
    return pl.pallas_call(
        functools.partial(project_kernel, parts),
        out_shape=tuple(
            jax.ShapeDtypeStruct((count, WIDTH), jnp.float32 if lo == 0 else jnp.bfloat16)
            for _, lo, count in parts
        ),
        in_specs=[VMEM, HBM],
        out_specs=(VMEM,) * len(parts),
        scratch_shapes=[
            pltpu.VMEM((chunks, w.shape[0], WIDTH), w.dtype),
            pltpu.SemaphoreType.DMA((chunks,)),
        ],
        compiler_params=pltpu.CompilerParams(vmem_limit_bytes=52 * 1024 * 1024),
        cost_estimate=pl.CostEstimate(
            flops=sum(2 * count * WIDTH * w.shape[0] for _, _, count in parts),
            bytes_accessed=4_000_000,
            transcendentals=0,
        ),
    )(rows, w)


def project(rows, w):
    chunks = w.shape[1] // WIDTH
    sides = lambda k: [(k, 2 * ROWS, ROWS), (k, 3 * ROWS, ROWS)]
    own = lambda k: [(k, 0, 2 * ROWS)]
    first = project_parts(rows, w, sides(0))
    rest = project_parts(rows, w, sum([sides(k) for k in range(1, chunks)], []))
    owns = project_parts(rows, w, sum([own(k) for k in range(chunks)], []))
    sent = first + rest
    return sent[0::2], sent[1::2], owns


def main_keys(rows):
    runs = rows.reshape(3, 2, RUN, 4, 4, HEAD).transpose(4, 1, 3, 0, 2, 5)
    return runs.reshape(32, MAIN, HEAD)


def shared_keys(rows, xl, c):
    runs = jnp.pad(rows, ((0, 32), (0, 0), (0, 0))).reshape(8, RUN, 4, HEAD)
    runs = jnp.where(xl == 0, runs, jnp.roll(runs, -4, axis=0))
    runs = jnp.where(c == 0, runs, jnp.roll(runs, -2, axis=0))
    return runs.transpose(0, 2, 1, 3).reshape(32, EXT, HEAD)


def merge(shares, levels):
    weights = jnp.exp2(levels - jnp.max(levels, axis=1, keepdims=True))
    weights = weights / jnp.sum(weights, axis=1, keepdims=True)
    return jnp.sum(shares.astype(jnp.float32) * weights[..., None], axis=1).astype(jnp.bfloat16)


def per_device(queries, key_rows, value_rows, block_list, block_count, w_out):
    xh, zh, zl, y, xl, c = [lax.axis_index(name) for name in NAMES]
    u = 2 * xl + c
    j = 2 * xh + zh
    k5 = key_rows.reshape(ROWS, 4, 5, HEAD)
    v5 = value_rows.reshape(ROWS, 4, 5, HEAD)
    q5 = queries.reshape(ROWS, 4, 5, HEAD)
    sent = jnp.concatenate(
        [
            main_keys(k5[:, :, :4]),
            shared_keys(k5[:, :, 4], xl, c),
            main_keys(v5[:, :, :4]),
            shared_keys(v5[:, :, 4], xl, c),
        ],
        axis=1,
    )
    kv = lax.all_to_all(sent, SPREAD, 0, 0, tiled=True).reshape(COLS, CHUNKS, KV, HEAD)

    q = jnp.stack([q5[:, :, :4], jnp.broadcast_to(q5[:, :, 4:], (ROWS, 4, 4, HEAD))])
    q = jnp.broadcast_to(q.transpose(3, 2, 0, 1, 4)[:, None], (4, 2, 4, 2, ROWS, HEAD))
    q = lax.all_to_all(q.reshape(32, 2, ROWS, HEAD), SPREAD, 0, 0, tiled=True)
    q = q.reshape(COLS, CHUNKS, 2, ROWS, HEAD).transpose(2, 0, 1, 3, 4).reshape(2 * UNITS, BLOCK, HEAD)

    where = jnp.stack([y, 5 * u + j, 5 * u + 4, 2 * j + zl, xl]).astype(jnp.int32)
    plans = plan(where, block_count, block_list)

    below, above = ring_up(kv), ring_down(kv)
    below, above, q, plans = lax.optimization_barrier((below, above, q, plans))
    last_k = ring_down(above[:, :, :PART])
    last_v = ring_up(below[:, :, PART:])
    state = attend(False, where, plans, q, (), (kv, below, above))
    out = attend(True, where, plans, q, state, (last_k, last_v))
    out = lax.all_to_all(out, ("xh", "zh", "zl"), 0, 0, tiled=True)

    levels = out[:, 2 * SUPER :].reshape(COLS, 3, STATS, BLOCK)[:, :, :6].astype(jnp.float32)
    levels = jnp.sum(levels.reshape(COLS, 3, 2, 3, BLOCK), axis=3).transpose(2, 0, 1, 3)
    levels = levels.reshape(2, COLS, SUPER)
    levels = jnp.where(xl == 0, levels, jnp.roll(levels, 2 * ROWS, axis=2))
    heads = merge(out[:, :SUPER].reshape(4, 2, SUPER, HEAD), levels[0].reshape(4, 2, SUPER))
    shared = merge(out[None, :, SUPER : 2 * SUPER], levels[1][None])
    attended = jnp.concatenate([heads, shared], axis=0).transpose(1, 0, 2).reshape(SUPER, 5 * HEAD)

    lows, highs, owns = project(attended, w_out)
    total = []
    for low, high, own in zip(lows, highs, owns):
        first = own[:ROWS] + around(low, -1).astype(jnp.float32)
        second = own[ROWS:] + around(high, 1).astype(jnp.float32)
        keep = jnp.where(c == 0, first, second)
        give = jnp.where(c == 0, second, first).astype(jnp.bfloat16)
        total.append((keep + lax.ppermute(give, "c", [(0, 1), (1, 0)])).astype(jnp.bfloat16))
    return jnp.concatenate(total, axis=1)


def solution(mesh):
    fine = Mesh(mesh.devices.reshape(SIZES), GRID)
    rows = P(NAMES, None)
    return jax.shard_map(
        per_device,
        mesh=fine,
        in_specs=(rows, rows, rows, P(), P(), P(("xl", "c"), None)),
        out_specs=rows,
        check_vma=False,
    )
```

```python
import functools

import jax
import jax.numpy as jnp
from jax import lax
from jax.experimental import pallas as pl
from jax.experimental.pallas import tpu as pltpu
from jax.sharding import Mesh, PartitionSpec as P

HEAD = 128
BLOCK = 128
ROWS = 96
CHUNKS = 4
SUPER = ROWS * CHUNKS
RUN = 16
MAIN = ROWS // 2
EXT = RUN
PART = MAIN + EXT
KV = 2 * PART
LOG2E = 1.4426950408889634
SCALE = HEAD ** -0.5 * LOG2E
FLOOR = -1e30
NAMES = ("xh", "zh", "zl", "y", "xl", "c")
GRID = ("xl", "c", "xh", "zh", "zl", "y")
SIZES = (2, 2, 2, 2, 2, 4)
SPREAD = ("xh", "zh", "zl", "xl", "c")
COLS = 8
UNITS = 3 * COLS
SLOTS = 16
MAIN_GROUP = 4
EXT_GROUP = 8
BATCH = 12
STATS = 16
BANDS = 4
WIDTHS = (1280, 1280, 1280, 1280)
SMEM = pl.BlockSpec(memory_space=pltpu.SMEM)
VMEM = pl.BlockSpec(memory_space=pltpu.VMEM)
HBM = pl.BlockSpec(memory_space=pl.ANY)


def ring_up(x):
    return lax.ppermute(x, "y", [(i, (i + 1) % 4) for i in range(4)])


def ring_down(x):
    return lax.ppermute(x, "y", [(i, (i - 1) % 4) for i in range(4)])


def plan_kernel(where_ref, counts_ref, table_ref, start_ref, n_ref, lists, sem):
    y, head, shared, share = [where_ref[i] for i in range(4)]
    copies = [
        pltpu.make_async_copy(table_ref.at[h], lists.at[i], sem.at[i])
        for i, h in enumerate((head, shared))
    ]
    for copy in copies:
        copy.start()
    for copy in copies:
        copy.wait()
    slots = lax.broadcasted_iota(jnp.int32, (SLOTS, lists.shape[2]), 0)
    for which, h in enumerate((head, shared)):
        block = lists[which]
        sb = (block * 171) >> 9
        r = block - 3 * sb
        dy = ((sb & 3) + 4 - y) & 3
        late = dy == 2
        place = jnp.where(late, 0, (4 - dy) & 3) - jnp.where(dy == 1, 1, 0)
        place = place * COLS + (sb >> 2)
        if which == 0:
            start = place * (CHUNKS * MAIN) + r * (BLOCK // 2)
        else:
            chunk = ((r * 8 + share) * 43) >> 8
            start = (place * CHUNKS + chunk) * EXT
        live = slots < counts_ref[pl.ds(h, 1), :]
        for stage in range(2):
            mine = jnp.where(live & (late == (stage == 1)), 1, 0)
            found = jnp.zeros((1, block.shape[1]), jnp.int32)
            sorted_ = jnp.zeros_like(block)
            for i in range(SLOTS):
                here = mine[i : i + 1]
                at = jnp.where(here == 1, found, SLOTS)
                sorted_ = jnp.where(slots == at, start[i : i + 1], sorted_)
                found = found + here
            start_ref[pl.ds((2 * which + stage) * SLOTS, SLOTS), :] = sorted_
            n_ref[pl.ds(2 * which + stage, 1), :] = found


def plan(where, counts, table):
    rows = counts.shape[1]
    return pl.pallas_call(
        plan_kernel,
        out_shape=(
            jax.ShapeDtypeStruct((4 * SLOTS, rows), jnp.int32),
            jax.ShapeDtypeStruct((4, rows), jnp.int32),
        ),
        in_specs=[SMEM, VMEM, HBM],
        out_specs=(VMEM, VMEM),
        scratch_shapes=[pltpu.VMEM((2, SLOTS, rows), jnp.int32), pltpu.SemaphoreType.DMA((2,))],
        cost_estimate=pl.CostEstimate(flops=1_000_000, bytes_accessed=100_000, transcendentals=0),
    )(where, counts, table.transpose(0, 2, 1))


def stage_kernel(last, pieces, *refs):
    where_ref, start_ref, n_ref, q_ref = refs[:4]
    refs = refs[4:]
    y, xl = where_ref[0], where_ref[4]
    if last:
        before, (last_k, last_v, out_ref), refs = refs[:3], refs[3:6], refs[6:]
        k_main, v_main, k_ext, v_ext, sem, top_ref, tot_ref, acc_ref = refs
        loads = [(last_k, 0, 0, k_main, k_ext), (last_v, 0, 0, v_main, v_ext)]
    else:
        sources, refs = refs[:pieces], refs[pieces:]
        top_ref, tot_ref, acc_ref, k_main, v_main, k_ext, v_ext, sem = refs
        loads = []
        for i, source in enumerate(sources):
            loads += [(source, 0, i, k_main, k_ext), (source, PART, i, v_main, v_ext)]
    stage = 1 if last else 0
    first = not last
    state = (top_ref, tot_ref, acc_ref)
    copies = []
    for source, lo, piece, main, ext in loads:
        for target, at, rows in ((main, lo, MAIN), (ext, lo + MAIN, EXT)):
            copy = pltpu.make_async_copy(
                source.at[:, :, pl.ds(at, rows)], target.at[piece], sem.at[len(copies)]
            )
            copy.start()
            copies.append(copy)

    for copy in copies:
        copy.wait()

    k_flat = k_main.reshape(pieces * COLS * CHUNKS * MAIN, HEAD)
    v_flat = v_main.reshape(pieces * COLS * CHUNKS * MAIN, HEAD)
    ke_flat = k_ext.reshape(pieces * COLS * CHUNKS * EXT, HEAD)
    ve_flat = v_ext.reshape(pieces * COLS * CHUNKS * EXT, HEAD)
    lane = lax.broadcasted_iota(jnp.int32, (BLOCK, HEAD), 1)
    eye = lax.broadcasted_iota(jnp.int32, (BLOCK, BLOCK), 0) == lane

    def dot_t(a, b):
        return lax.dot_general(a, b, (((1,), (1,)), ((), ())), preferred_element_type=jnp.float32)

    def run(units, group, key_flat, value_flat, width):
        lists = [2 * (unit // UNITS) + stage for unit in units]
        rows = [3 * y + 12 * (unit % UNITS // 3) + unit % 3 for unit in units]
        ns = [n_ref[i, row] for i, row in zip(lists, rows)]
        most = functools.reduce(jnp.maximum, ns)

        def step(t, carry, start=False):
            col = lax.broadcasted_iota(jnp.int32, (1, group * width), 1)
            values, scores = [], []
            for unit, n, which, row in zip(units, ns, lists, rows):
                starts = []
                for i in range(group):
                    slot = jnp.maximum(jnp.minimum(group * t + i, n - 1), 0)
                    at = start_ref[which * SLOTS + slot, row]
                    starts.append(pl.multiple_of(at, width))
                keys = jnp.concatenate([key_flat[pl.ds(r, width), :] for r in starts], axis=0)
                values.append(
                    jnp.concatenate([value_flat[pl.ds(r, width), :] for r in starts], axis=0)
                )
                bias = jnp.where(col < (n - group * t) * width, 0.0, 2 * FLOOR)
                scores.append(dot_t(q_ref[unit], keys) + bias)
            for unit, s, v in zip(units, scores, values):
                parts = [s[:, i : i + HEAD] for i in range(0, group * width, HEAD)]
                peak = jnp.max(functools.reduce(jnp.maximum, parts), axis=1, keepdims=True)
                if start and first:
                    new_top = jnp.maximum(jnp.broadcast_to(peak, (BLOCK, HEAD)), FLOOR)
                else:
                    top, tot, acc = [ref[unit] for ref in (before if start else state)]
                    new_top = jnp.maximum(top, peak)
                weights = [jnp.exp2((part - new_top) * SCALE) for part in parts]
                low = jnp.concatenate([w.astype(jnp.bfloat16) for w in weights], axis=1)
                product = jnp.dot(low, v, preferred_element_type=jnp.float32)
                total = functools.reduce(jnp.add, weights)
                if not (start and first):
                    alpha = jnp.exp2((top - new_top) * SCALE)
                    total = tot * alpha + total
                    product = acc * alpha + product
                top_ref[unit] = new_top
                tot_ref[unit] = total
                acc_ref[unit] = product
            return carry

        step(0, 0, True)
        lax.fori_loop(1, lax.div(most + (group - 1), group), step, 0)

    def finish(unit):
        total = jnp.sum(tot_ref[unit], axis=1, keepdims=True)
        return top_ref[unit], total, (acc_ref[unit] / total).astype(jnp.bfloat16)

    def store(sb, r, top, value):
        for i in range(4):
            granule = 4 * r + i
            chunk = granule // 3
            to = sb if chunk in (0, 3) else jnp.where(xl == 2 - chunk, sb ^ 4, sb)
            place = lax.rem(chunk + 4 - 2 * xl, 4)
            row = pl.multiple_of(top + place * ROWS + (granule % 3) * 32, 32)
            out_ref[to, pl.ds(row, 32), :] = value[32 * i : 32 * i + 32]

    levels = [[], []]
    for which in range(2):
        for lo in range(0, UNITS, BATCH):
            units = range(which * UNITS + lo, which * UNITS + lo + BATCH)
            if which == 0:
                run(units, MAIN_GROUP, k_flat, v_flat, BLOCK // 2)
            else:
                run(units, EXT_GROUP, ke_flat, ve_flat, RUN)
            if not last:
                continue
            for unit in units:
                top, total, value = finish(unit)
                local = unit - which * UNITS
                store(local // 3, local % 3, which * SUPER, value)
                level = top * SCALE + jnp.log2(total)
                levels[which].append(jnp.sum(jnp.where(eye, level, 0.0), axis=0, keepdims=True))
    if not last:
        return
    index = lax.broadcasted_iota(jnp.int32, (STATS, HEAD), 0)
    column = lax.broadcasted_iota(jnp.int32, (1, HEAD), 1)
    for unit in range(UNITS):
        sb, r = unit // 3, unit % 3
        chunk = (r * BLOCK + column) // ROWS
        tile = jnp.zeros((STATS, HEAD), jnp.float32)
        for which in range(2):
            level = jnp.where(chunk == 2 - xl, levels[which][3 * (sb ^ 4) + r], levels[which][unit])
            for i in range(3):
                term = level.astype(jnp.bfloat16).astype(jnp.float32)
                tile = jnp.where(index == 3 * which + i, term, tile)
                level = level - term
        out_ref[sb, pl.ds(2 * SUPER + r * STATS, STATS), :] = tile.astype(jnp.bfloat16)


def attend(last, where, plans, q, state, sources):
    pieces = 1 if last else len(sources)
    kept = jax.ShapeDtypeStruct((2 * UNITS, BLOCK, HEAD), jnp.float32)
    scratch = [
        pltpu.VMEM((pieces, COLS, CHUNKS, MAIN, HEAD), jnp.bfloat16),
        pltpu.VMEM((pieces, COLS, CHUNKS, MAIN, HEAD), jnp.bfloat16),
        pltpu.VMEM((pieces, COLS, CHUNKS, EXT, HEAD), jnp.bfloat16),
        pltpu.VMEM((pieces, COLS, CHUNKS, EXT, HEAD), jnp.bfloat16),
        pltpu.SemaphoreType.DMA((4 * pieces,)),
    ]
    if last:
        out_shape = jax.ShapeDtypeStruct((COLS, 2 * SUPER + 3 * STATS, HEAD), jnp.bfloat16)
        out_specs = VMEM
        scratch += [pltpu.VMEM(kept.shape, kept.dtype)] * 3
    else:
        out_shape, out_specs = (kept,) * 3, (VMEM,) * 3
    return pl.pallas_call(
        functools.partial(stage_kernel, last, pieces),
        out_shape=out_shape,
        in_specs=[SMEM] * 3 + [VMEM] * (1 + len(state)) + [HBM] * len(sources),
        out_specs=out_specs,
        scratch_shapes=scratch,
        compiler_params=pltpu.CompilerParams(vmem_limit_bytes=32 * 1024 * 1024),
        cost_estimate=pl.CostEstimate(
            flops=pieces * 5_000_000_000, bytes_accessed=pieces * 2_000_000, transcendentals=1_000_000
        ),
    )(where, *plans, q, *state, *sources)


def around(x, step):
    index = lambda at: (at % 2) * 2 + at % 4 // 2
    return lax.ppermute(x, ("xl", "xh"), [(index(i), index(i + step)) for i in range(4)])


def project_kernel(parts, rows_ref, w_ref, *refs):
    chunks = sorted({chunk for chunk, _, _ in parts})
    outs, bufs, sem = refs[: len(parts)], refs[len(parts) : -1], refs[-1]
    copies = []
    for i, (chunk, buf) in enumerate(zip(chunks, bufs)):
        columns = pl.ds(sum(WIDTHS[:chunk]), WIDTHS[chunk])
        band = buf.shape[0] // BANDS
        copies.append([])
        for j in range(BANDS):
            rows = pl.ds(j * band, band)
            copy = pltpu.make_async_copy(w_ref.at[rows, columns], buf.at[rows], sem.at[i, j])
            copy.start()
            copies[-1].append(copy)
    for chunk, buf, bands in zip(chunks, bufs, copies):
        for copy in bands:
            copy.wait()
        for (which, lo, count), out in zip(parts, outs):
            if which != chunk:
                continue
            rows = rows_ref[pl.ds(lo, count), :]
            for at in range(0, WIDTHS[chunk], 256):
                columns = pl.ds(at, min(256, WIDTHS[chunk] - at))
                product = jnp.dot(rows, buf[:, columns], preferred_element_type=jnp.float32)
                out[:, columns] = product.astype(out.dtype)


def project_parts(rows, w, parts):
    chunks = sorted({chunk for chunk, _, _ in parts})
    return pl.pallas_call(
        functools.partial(project_kernel, parts),
        out_shape=tuple(
            jax.ShapeDtypeStruct((count, WIDTHS[chunk]), jnp.float32 if lo == 0 else jnp.bfloat16)
            for chunk, lo, count in parts
        ),
        in_specs=[VMEM, HBM],
        out_specs=(VMEM,) * len(parts),
        scratch_shapes=[
            *[pltpu.VMEM((w.shape[0], WIDTHS[chunk]), w.dtype) for chunk in chunks],
            pltpu.SemaphoreType.DMA((len(chunks), BANDS)),
        ],
        compiler_params=pltpu.CompilerParams(vmem_limit_bytes=52 * 1024 * 1024),
        cost_estimate=pl.CostEstimate(
            flops=sum(2 * count * WIDTHS[chunk] * w.shape[0] for chunk, _, count in parts),
            bytes_accessed=4_000_000,
            transcendentals=0,
        ),
    )(rows, w)


def project(rows, w):
    chunks = len(WIDTHS)
    sides = lambda k: [(k, 2 * ROWS, ROWS), (k, 3 * ROWS, ROWS)]
    own = lambda k: [(k, 0, 2 * ROWS)]
    low, high, head = project_parts(rows, w, sides(0) + own(0))
    rest = project_parts(rows, w, sum([sides(k) for k in range(1, chunks)], []))
    owns = project_parts(rows, w, sum([own(k) for k in range(1, chunks)], []))
    return (low,) + rest[0::2], (high,) + rest[1::2], (head,) + owns


def pack_kv_kernel(chunk_ref, k_ref, v_ref, out_ref):
    for j in range(4):
        for e in range(2):
            run = (2 * j + e + 2 * chunk_ref[0]) & 7
            row = pl.multiple_of(jnp.minimum(run, 5) * RUN, RUN)
            for u in range(4):
                group = (2 * j + e) * 4 + u
                for lo, ref in ((0, k_ref), (PART, v_ref)):
                    head = pl.ds((5 * u + j) * HEAD, HEAD)
                    for i in range(3):
                        out_ref[group, pl.ds(lo + i * RUN, RUN), :] = ref[pl.ds((2 * i + e) * RUN, RUN), head]
                    shared = ref[pl.ds(row, RUN), pl.ds((5 * u + 4) * HEAD, HEAD)]
                    out_ref[group, pl.ds(lo + MAIN, EXT), :] = shared


def pack_kv(chunk, k, v):
    return pl.pallas_call(
        pack_kv_kernel,
        out_shape=jax.ShapeDtypeStruct((32, KV, HEAD), k.dtype),
        in_specs=[SMEM, VMEM, VMEM],
        out_specs=VMEM,
        cost_estimate=pl.CostEstimate(flops=1_000_000, bytes_accessed=2_000_000, transcendentals=0),
    )(chunk.reshape(1), k, v)


def pack_q_kernel(q_ref, out_ref):
    for u in range(4):
        for j in range(4):
            for which, head in enumerate((5 * u + j, 5 * u + 4)):
                rows = q_ref[:, pl.ds(head * HEAD, HEAD)]
                for e in range(2):
                    out_ref[(2 * j + e) * 4 + u, which] = rows


def pack_q(q):
    return pl.pallas_call(
        pack_q_kernel,
        out_shape=jax.ShapeDtypeStruct((32, 2, ROWS, HEAD), q.dtype),
        in_specs=[VMEM],
        out_specs=VMEM,
        cost_estimate=pl.CostEstimate(flops=1_000_000, bytes_accessed=2_000_000, transcendentals=0),
    )(q)


def merge(shares, levels):
    weights = jnp.exp2(levels - jnp.max(levels, axis=1, keepdims=True))
    weights = weights / jnp.sum(weights, axis=1, keepdims=True)
    return jnp.sum(shares.astype(jnp.float32) * weights[..., None], axis=1).astype(jnp.bfloat16)


def per_device(queries, key_rows, value_rows, block_list, block_count, w_out):
    xh, zh, zl, y, xl, c = [lax.axis_index(name) for name in NAMES]
    u = 2 * xl + c
    j = 2 * xh + zh
    sent = pack_kv((2 * xl + c).astype(jnp.int32), key_rows, value_rows)
    kv = lax.all_to_all(sent, SPREAD, 0, 0, tiled=True).reshape(COLS, CHUNKS, KV, HEAD)
    q = lax.all_to_all(pack_q(queries), SPREAD, 0, 0, tiled=True)
    q = q.reshape(COLS, CHUNKS, 2, ROWS, HEAD).transpose(2, 0, 1, 3, 4).reshape(2 * UNITS, BLOCK, HEAD)

    where = jnp.stack([y, 5 * u + j, 5 * u + 4, 2 * j + zl, xl]).astype(jnp.int32)
    plans = plan(where, block_count, block_list)

    below, above = ring_up(kv), ring_down(kv)
    below, above, q, plans = lax.optimization_barrier((below, above, q, plans))
    last_k = ring_down(above[:, :, :PART])
    last_v = ring_up(below[:, :, PART:])
    state = attend(False, where, plans, q, (), (kv, below, above))
    out = attend(True, where, plans, q, state, (last_k, last_v))
    out = lax.all_to_all(out, ("xh", "zh", "zl"), 0, 0, tiled=True)
    out, w_out, xl, c = lax.optimization_barrier((out, w_out, xl, c))

    levels = out[:, 2 * SUPER :].reshape(COLS, 3, STATS, BLOCK)[:, :, :6].astype(jnp.float32)
    levels = jnp.sum(levels.reshape(COLS, 3, 2, 3, BLOCK), axis=3).transpose(2, 0, 1, 3)
    levels = levels.reshape(2, COLS, SUPER)
    levels = jnp.where(xl == 0, levels, jnp.roll(levels, 2 * ROWS, axis=2))
    heads = merge(out[:, :SUPER].reshape(4, 2, SUPER, HEAD), levels[0].reshape(4, 2, SUPER))
    shared = merge(out[None, :, SUPER : 2 * SUPER], levels[1][None])
    attended = jnp.concatenate([heads, shared], axis=0).transpose(1, 0, 2).reshape(SUPER, 5 * HEAD)

    lows, highs, owns = project(attended, w_out)
    total = []
    for low, high, own in zip(lows, highs, owns):
        first = own[:ROWS] + around(low, -1).astype(jnp.float32)
        second = own[ROWS:] + around(high, 1).astype(jnp.float32)
        keep = jnp.where(c == 0, first, second)
        give = jnp.where(c == 0, second, first).astype(jnp.bfloat16)
        total.append((keep + lax.ppermute(give, "c", [(0, 1), (1, 0)])).astype(jnp.bfloat16))
    return jnp.concatenate(total, axis=1)


def solution(mesh):
    fine = Mesh(mesh.devices.reshape(SIZES), GRID)
    rows = P(NAMES, None)
    return jax.shard_map(
        per_device,
        mesh=fine,
        in_specs=(rows, rows, rows, P(), P(), P(("xl", "c"), None)),
        out_specs=rows,
        check_vma=False,
    )
```

```python
import functools

import jax
import jax.numpy as jnp
from jax import lax
from jax.experimental import pallas as pl
from jax.experimental.pallas import tpu as pltpu
from jax.sharding import Mesh, PartitionSpec as P

HEAD = 128
BLOCK = 128
ROWS = 96
CHUNKS = 4
SUPER = ROWS * CHUNKS
RUN = 16
MAIN = ROWS // 2
EXT = RUN
PART = MAIN + EXT
KV = 2 * PART
LOG2E = 1.4426950408889634
SCALE = HEAD ** -0.5 * LOG2E
FLOOR = -1e30
NAMES = ("xh", "zh", "zl", "y", "xl", "c")
GRID = ("xl", "c", "xh", "zh", "zl", "y")
SIZES = (2, 2, 2, 2, 2, 4)
SPREAD = ("xh", "zh", "zl", "xl", "c")
COLS = 8
UNITS = 3 * COLS
SLOTS = 16
MAIN_GROUP = 4
EXT_GROUP = 8
BATCH = 12
STATS = 16
BANDS = 4
WIDTHS = (1280, 1280, 1280, 1280)
SMEM = pl.BlockSpec(memory_space=pltpu.SMEM)
VMEM = pl.BlockSpec(memory_space=pltpu.VMEM)
HBM = pl.BlockSpec(memory_space=pl.ANY)


def ring_up(x):
    return lax.ppermute(x, "y", [(i, (i + 1) % 4) for i in range(4)])


def ring_down(x):
    return lax.ppermute(x, "y", [(i, (i - 1) % 4) for i in range(4)])


def plan_kernel(where_ref, counts_ref, table_ref, start_ref, n_ref, lists, sem):
    y, head, shared, share = [where_ref[i] for i in range(4)]
    copies = [
        pltpu.make_async_copy(table_ref.at[h], lists.at[i], sem.at[i])
        for i, h in enumerate((head, shared))
    ]
    for copy in copies:
        copy.start()
    for copy in copies:
        copy.wait()
    slots = lax.broadcasted_iota(jnp.int32, (SLOTS, lists.shape[2]), 0)
    for which, h in enumerate((head, shared)):
        block = lists[which]
        sb = (block * 171) >> 9
        r = block - 3 * sb
        dy = ((sb & 3) + 4 - y) & 3
        late = dy == 2
        place = jnp.where(late, 0, (4 - dy) & 3) - jnp.where(dy == 1, 1, 0)
        place = place * COLS + (sb >> 2)
        if which == 0:
            start = place * (CHUNKS * MAIN) + r * (BLOCK // 2)
        else:
            chunk = ((r * 8 + share) * 43) >> 8
            start = (place * CHUNKS + chunk) * EXT
        live = slots < counts_ref[pl.ds(h, 1), :]
        for stage in range(2):
            mine = jnp.where(live & (late == (stage == 1)), 1, 0)
            found = jnp.zeros((1, block.shape[1]), jnp.int32)
            sorted_ = jnp.zeros_like(block)
            for i in range(SLOTS):
                here = mine[i : i + 1]
                at = jnp.where(here == 1, found, SLOTS)
                sorted_ = jnp.where(slots == at, start[i : i + 1], sorted_)
                found = found + here
            start_ref[pl.ds((2 * which + stage) * SLOTS, SLOTS), :] = sorted_
            n_ref[pl.ds(2 * which + stage, 1), :] = found


def plan(where, counts, table):
    rows = counts.shape[1]
    return pl.pallas_call(
        plan_kernel,
        out_shape=(
            jax.ShapeDtypeStruct((4 * SLOTS, rows), jnp.int32),
            jax.ShapeDtypeStruct((4, rows), jnp.int32),
        ),
        in_specs=[SMEM, VMEM, HBM],
        out_specs=(VMEM, VMEM),
        scratch_shapes=[pltpu.VMEM((2, SLOTS, rows), jnp.int32), pltpu.SemaphoreType.DMA((2,))],
        cost_estimate=pl.CostEstimate(flops=1_000_000, bytes_accessed=100_000, transcendentals=0),
    )(where, counts, table.transpose(0, 2, 1))


def stage_kernel(last, pieces, *refs):
    where_ref, start_ref, n_ref, q_ref = refs[:4]
    refs = refs[4:]
    y, xl = where_ref[0], where_ref[4]
    if last:
        before, (last_k, last_v, out_ref), refs = refs[:3], refs[3:6], refs[6:]
        k_main, v_main, k_ext, v_ext, sem, top_ref, tot_ref, acc_ref = refs
        loads = [(last_k, 0, 0, k_main, k_ext), (last_v, 0, 0, v_main, v_ext)]
    else:
        sources, refs = refs[:pieces], refs[pieces:]
        top_ref, tot_ref, acc_ref, k_main, v_main, k_ext, v_ext, sem = refs
        loads = []
        for i, source in enumerate(sources):
            loads += [(source, 0, i, k_main, k_ext), (source, PART, i, v_main, v_ext)]
    stage = 1 if last else 0
    first = not last
    state = (top_ref, tot_ref, acc_ref)
    copies = []
    for source, lo, piece, main, ext in loads:
        for target, at, rows in ((main, lo, MAIN), (ext, lo + MAIN, EXT)):
            copy = pltpu.make_async_copy(
                source.at[:, :, pl.ds(at, rows)], target.at[piece], sem.at[len(copies)]
            )
            copy.start()
            copies.append(copy)

    for copy in copies:
        copy.wait()

    k_flat = k_main.reshape(pieces * COLS * CHUNKS * MAIN, HEAD)
    v_flat = v_main.reshape(pieces * COLS * CHUNKS * MAIN, HEAD)
    ke_flat = k_ext.reshape(pieces * COLS * CHUNKS * EXT, HEAD)
    ve_flat = v_ext.reshape(pieces * COLS * CHUNKS * EXT, HEAD)
    lane = lax.broadcasted_iota(jnp.int32, (BLOCK, HEAD), 1)
    eye = lax.broadcasted_iota(jnp.int32, (BLOCK, BLOCK), 0) == lane

    def dot_t(a, b):
        return lax.dot_general(a, b, (((1,), (1,)), ((), ())), preferred_element_type=jnp.float32)

    def run(units, group, key_flat, value_flat, width):
        lists = [2 * (unit // UNITS) + stage for unit in units]
        rows = [3 * y + 12 * (unit % UNITS // 3) + unit % 3 for unit in units]
        ns = [n_ref[i, row] for i, row in zip(lists, rows)]
        most = functools.reduce(jnp.maximum, ns)

        def step(t, carry, start=False):
            col = lax.broadcasted_iota(jnp.int32, (1, group * width), 1)
            values, scores = [], []
            for unit, n, which, row in zip(units, ns, lists, rows):
                starts = []
                for i in range(group):
                    slot = jnp.maximum(jnp.minimum(group * t + i, n - 1), 0)
                    at = start_ref[which * SLOTS + slot, row]
                    starts.append(pl.multiple_of(at, width))
                keys = jnp.concatenate([key_flat[pl.ds(r, width), :] for r in starts], axis=0)
                values.append(
                    jnp.concatenate([value_flat[pl.ds(r, width), :] for r in starts], axis=0)
                )
                bias = jnp.where(col < (n - group * t) * width, 0.0, 2 * FLOOR)
                scores.append(dot_t(q_ref[unit], keys) + bias)
            for unit, s, v in zip(units, scores, values):
                parts = [s[:, i : i + HEAD] for i in range(0, group * width, HEAD)]
                peak = jnp.max(functools.reduce(jnp.maximum, parts), axis=1, keepdims=True)
                if start and first:
                    new_top = jnp.maximum(jnp.broadcast_to(peak, (BLOCK, HEAD)), FLOOR)
                else:
                    top, tot, acc = [ref[unit] for ref in (before if start else state)]
                    new_top = jnp.maximum(top, peak)
                weights = [jnp.exp2((part - new_top) * SCALE) for part in parts]
                low = jnp.concatenate([w.astype(jnp.bfloat16) for w in weights], axis=1)
                product = jnp.dot(low, v, preferred_element_type=jnp.float32)
                total = functools.reduce(jnp.add, weights)
                if not (start and first):
                    alpha = jnp.exp2((top - new_top) * SCALE)
                    total = tot * alpha + total
                    product = acc * alpha + product
                top_ref[unit] = new_top
                tot_ref[unit] = total
                acc_ref[unit] = product
            return carry

        step(0, 0, True)
        lax.fori_loop(1, lax.div(most + (group - 1), group), step, 0)

    def finish(unit):
        total = jnp.sum(tot_ref[unit], axis=1, keepdims=True)
        return top_ref[unit], total, (acc_ref[unit] / total).astype(jnp.bfloat16)

    def store(sb, r, top, value):
        for i in range(4):
            granule = 4 * r + i
            chunk = granule // 3
            to = sb if chunk in (0, 3) else jnp.where(xl == 2 - chunk, sb ^ 4, sb)
            place = lax.rem(chunk + 4 - 2 * xl, 4)
            row = pl.multiple_of(top + place * ROWS + (granule % 3) * 32, 32)
            out_ref[to, pl.ds(row, 32), :] = value[32 * i : 32 * i + 32]

    levels = [[], []]
    for which in range(2):
        for lo in range(0, UNITS, BATCH):
            units = range(which * UNITS + lo, which * UNITS + lo + BATCH)
            if which == 0:
                run(units, MAIN_GROUP, k_flat, v_flat, BLOCK // 2)
            else:
                run(units, EXT_GROUP, ke_flat, ve_flat, RUN)
            if not last:
                continue
            for unit in units:
                top, total, value = finish(unit)
                local = unit - which * UNITS
                store(local // 3, local % 3, which * SUPER, value)
                level = top * SCALE + jnp.log2(total)
                levels[which].append(jnp.sum(jnp.where(eye, level, 0.0), axis=0, keepdims=True))
    if not last:
        return
    index = lax.broadcasted_iota(jnp.int32, (STATS, HEAD), 0)
    column = lax.broadcasted_iota(jnp.int32, (1, HEAD), 1)
    for unit in range(UNITS):
        sb, r = unit // 3, unit % 3
        chunk = (r * BLOCK + column) // ROWS
        tile = jnp.zeros((STATS, HEAD), jnp.float32)
        for which in range(2):
            level = jnp.where(chunk == 2 - xl, levels[which][3 * (sb ^ 4) + r], levels[which][unit])
            for i in range(3):
                term = level.astype(jnp.bfloat16).astype(jnp.float32)
                tile = jnp.where(index == 3 * which + i, term, tile)
                level = level - term
        out_ref[sb, pl.ds(2 * SUPER + r * STATS, STATS), :] = tile.astype(jnp.bfloat16)


def attend(last, where, plans, q, state, sources):
    pieces = 1 if last else len(sources)
    kept = jax.ShapeDtypeStruct((2 * UNITS, BLOCK, HEAD), jnp.float32)
    scratch = [
        pltpu.VMEM((pieces, COLS, CHUNKS, MAIN, HEAD), jnp.bfloat16),
        pltpu.VMEM((pieces, COLS, CHUNKS, MAIN, HEAD), jnp.bfloat16),
        pltpu.VMEM((pieces, COLS, CHUNKS, EXT, HEAD), jnp.bfloat16),
        pltpu.VMEM((pieces, COLS, CHUNKS, EXT, HEAD), jnp.bfloat16),
        pltpu.SemaphoreType.DMA((4 * pieces,)),
    ]
    if last:
        out_shape = jax.ShapeDtypeStruct((COLS, 2 * SUPER + 3 * STATS, HEAD), jnp.bfloat16)
        out_specs = VMEM
        scratch += [pltpu.VMEM(kept.shape, kept.dtype)] * 3
    else:
        out_shape, out_specs = (kept,) * 3, (VMEM,) * 3
    return pl.pallas_call(
        functools.partial(stage_kernel, last, pieces),
        out_shape=out_shape,
        in_specs=[SMEM] * 3 + [VMEM] * (1 + len(state)) + [HBM] * len(sources),
        out_specs=out_specs,
        scratch_shapes=scratch,
        compiler_params=pltpu.CompilerParams(vmem_limit_bytes=32 * 1024 * 1024),
        cost_estimate=pl.CostEstimate(
            flops=pieces * 5_000_000_000, bytes_accessed=pieces * 2_000_000, transcendentals=1_000_000
        ),
    )(where, *plans, q, *state, *sources)


def around(x, step):
    index = lambda at: (at % 2) * 2 + at % 4 // 2
    return lax.ppermute(x, ("xl", "xh"), [(index(i), index(i + step)) for i in range(4)])


def project_kernel(parts, heads_ref, shared_ref, w_ref, *refs):
    chunks = sorted({chunk for chunk, _, _ in parts})
    outs, bufs, sem = refs[: len(parts)], refs[len(parts) : -1], refs[-1]
    copies = []
    for i, (chunk, buf) in enumerate(zip(chunks, bufs)):
        columns = pl.ds(sum(WIDTHS[:chunk]), WIDTHS[chunk])
        band = buf.shape[0] // BANDS
        copies.append([])
        for j in range(BANDS):
            rows = pl.ds(j * band, band)
            copy = pltpu.make_async_copy(w_ref.at[rows, columns], buf.at[rows], sem.at[i, j])
            copy.start()
            copies[-1].append(copy)
    for chunk, buf, bands in zip(chunks, bufs, copies):
        for copy in bands:
            copy.wait()
        for (which, lo, count), out in zip(parts, outs):
            if which != chunk:
                continue
            rows = [heads_ref[j, pl.ds(lo, count), :] for j in range(4)]
            rows = jnp.concatenate(rows + [shared_ref[0, pl.ds(lo, count), :]], axis=1)
            for at in range(0, WIDTHS[chunk], 256):
                columns = pl.ds(at, min(256, WIDTHS[chunk] - at))
                product = jnp.dot(rows, buf[:, columns], preferred_element_type=jnp.float32)
                out[:, columns] = product.astype(out.dtype)


def project_parts(rows, w, parts):
    chunks = sorted({chunk for chunk, _, _ in parts})
    return pl.pallas_call(
        functools.partial(project_kernel, parts),
        out_shape=tuple(
            jax.ShapeDtypeStruct((count, WIDTHS[chunk]), jnp.float32 if lo == 0 else jnp.bfloat16)
            for chunk, lo, count in parts
        ),
        in_specs=[VMEM, VMEM, HBM],
        out_specs=(VMEM,) * len(parts),
        scratch_shapes=[
            *[pltpu.VMEM((w.shape[0], WIDTHS[chunk]), w.dtype) for chunk in chunks],
            pltpu.SemaphoreType.DMA((len(chunks), BANDS)),
        ],
        compiler_params=pltpu.CompilerParams(vmem_limit_bytes=52 * 1024 * 1024),
        cost_estimate=pl.CostEstimate(
            flops=sum(2 * count * WIDTHS[chunk] * w.shape[0] for chunk, _, count in parts),
            bytes_accessed=4_000_000,
            transcendentals=0,
        ),
    )(*rows, w)


def project(rows, w):
    chunks = len(WIDTHS)
    sides = lambda k: [(k, 2 * ROWS, ROWS), (k, 3 * ROWS, ROWS)]
    own = lambda k: [(k, 0, 2 * ROWS)]
    low, high, head = project_parts(rows, w, sides(0) + own(0))
    rest = project_parts(rows, w, sum([sides(k) for k in range(1, chunks)], []))
    owns = project_parts(rows, w, sum([own(k) for k in range(1, chunks)], []))
    return (low,) + rest[0::2], (high,) + rest[1::2], (head,) + owns


def pack_kv_kernel(chunk_ref, k_ref, v_ref, out_ref):
    for j in range(4):
        for e in range(2):
            run = (2 * j + e + 2 * chunk_ref[0]) & 7
            row = pl.multiple_of(jnp.minimum(run, 5) * RUN, RUN)
            for u in range(4):
                group = (2 * j + e) * 4 + u
                for lo, ref in ((0, k_ref), (PART, v_ref)):
                    head = pl.ds((5 * u + j) * HEAD, HEAD)
                    for i in range(3):
                        out_ref[group, pl.ds(lo + i * RUN, RUN), :] = ref[pl.ds((2 * i + e) * RUN, RUN), head]
                    shared = ref[pl.ds(row, RUN), pl.ds((5 * u + 4) * HEAD, HEAD)]
                    out_ref[group, pl.ds(lo + MAIN, EXT), :] = shared


def pack_kv(chunk, k, v):
    return pl.pallas_call(
        pack_kv_kernel,
        out_shape=jax.ShapeDtypeStruct((32, KV, HEAD), k.dtype),
        in_specs=[SMEM, VMEM, VMEM],
        out_specs=VMEM,
        cost_estimate=pl.CostEstimate(flops=1_000_000, bytes_accessed=2_000_000, transcendentals=0),
    )(chunk.reshape(1), k, v)


def pack_q_kernel(q_ref, out_ref):
    for u in range(4):
        for j in range(4):
            for which, head in enumerate((5 * u + j, 5 * u + 4)):
                rows = q_ref[:, pl.ds(head * HEAD, HEAD)]
                for e in range(2):
                    out_ref[(2 * j + e) * 4 + u, which] = rows


def pack_q(q):
    return pl.pallas_call(
        pack_q_kernel,
        out_shape=jax.ShapeDtypeStruct((32, 2, ROWS, HEAD), q.dtype),
        in_specs=[VMEM],
        out_specs=VMEM,
        cost_estimate=pl.CostEstimate(flops=1_000_000, bytes_accessed=2_000_000, transcendentals=0),
    )(q)


def merge(shares, levels):
    weights = jnp.exp2(levels - jnp.max(levels, axis=1, keepdims=True))
    weights = weights / jnp.sum(weights, axis=1, keepdims=True)
    return jnp.sum(shares.astype(jnp.float32) * weights[..., None], axis=1).astype(jnp.bfloat16)


def per_device(queries, key_rows, value_rows, block_list, block_count, w_out):
    xh, zh, zl, y, xl, c = [lax.axis_index(name) for name in NAMES]
    u = 2 * xl + c
    j = 2 * xh + zh
    sent = pack_kv((2 * xl + c).astype(jnp.int32), key_rows, value_rows)
    kv = lax.all_to_all(sent, SPREAD, 0, 0, tiled=True).reshape(COLS, CHUNKS, KV, HEAD)
    q = lax.all_to_all(pack_q(queries), SPREAD, 0, 0, tiled=True)
    q = q.reshape(COLS, CHUNKS, 2, ROWS, HEAD).transpose(2, 0, 1, 3, 4).reshape(2 * UNITS, BLOCK, HEAD)

    where = jnp.stack([y, 5 * u + j, 5 * u + 4, 2 * j + zl, xl]).astype(jnp.int32)
    plans = plan(where, block_count, block_list)

    below, above = ring_up(kv), ring_down(kv)
    below, above, q, plans = lax.optimization_barrier((below, above, q, plans))
    last_k = ring_down(above[:, :, :PART])
    last_v = ring_up(below[:, :, PART:])
    state = attend(False, where, plans, q, (), (kv, below, above))
    out = attend(True, where, plans, q, state, (last_k, last_v))
    out = lax.all_to_all(out, ("xh", "zh", "zl"), 0, 0, tiled=True)
    out, w_out, xl, c = lax.optimization_barrier((out, w_out, xl, c))

    levels = out[:, 2 * SUPER :].reshape(COLS, 3, STATS, BLOCK)[:, :, :6].astype(jnp.float32)
    levels = jnp.sum(levels.reshape(COLS, 3, 2, 3, BLOCK), axis=3).transpose(2, 0, 1, 3)
    levels = levels.reshape(2, COLS, SUPER)
    levels = jnp.where(xl == 0, levels, jnp.roll(levels, 2 * ROWS, axis=2))
    heads = merge(out[:, :SUPER].reshape(4, 2, SUPER, HEAD), levels[0].reshape(4, 2, SUPER))
    shared = merge(out[None, :, SUPER : 2 * SUPER], levels[1][None])

    lows, highs, owns = project((heads, shared), w_out)
    total = []
    for low, high, own in zip(lows, highs, owns):
        first = own[:ROWS] + around(low, -1).astype(jnp.float32)
        second = own[ROWS:] + around(high, 1).astype(jnp.float32)
        keep = jnp.where(c == 0, first, second)
        give = jnp.where(c == 0, second, first).astype(jnp.bfloat16)
        total.append((keep + lax.ppermute(give, "c", [(0, 1), (1, 0)])).astype(jnp.bfloat16))
    return jnp.concatenate(total, axis=1)


def solution(mesh):
    fine = Mesh(mesh.devices.reshape(SIZES), GRID)
    rows = P(NAMES, None)
    return jax.shard_map(
        per_device,
        mesh=fine,
        in_specs=(rows, rows, rows, P(), P(), P(("xl", "c"), None)),
        out_specs=rows,
        check_vma=False,
    )
```
